256 devices in a mesh: dp: 8 (over z), expert: 32 (over x, y, core).
Axes of the slice: x: 4, y: 4, z: 8, core: 2. Of those that a mesh axis runs over, the one named last changes fastest.
Arguments:
- tokens: bfloat16 [32768, 4096], P(('dp', 'expert')), may hold values from -6 to 6
- latent_proj: bfloat16 [4096, 1024], P(('dp', 'expert')), may hold values from -0.09375 to 0.09375
- first_weight: bfloat16 [32, 1024, 1408], P('expert', 'dp'), may hold values from -0.1875 to 0.1875
- second_weight: bfloat16 [32, 1408, 1024], P('expert', 'dp'), may hold values from -0.15625 to 0.15625
- route_ids: int32 [32768, 4], P(('dp', 'expert')), may hold values from 0 to 31, all different within a row; in each aligned block of 128 rows (0 to 127, 128 to 255, ...) at most 24 rows name the same one
- gate_numer: int32 [32768, 4], P(('dp', 'expert')), may hold values from 1 to 256
- out_cotangent: bfloat16 [32768, 1024], P(('dp', 'expert')), may hold values from -6 to 6
Outputs:
- grad_tokens: bfloat16 [32768, 4096], P(('dp', 'expert'))
- first_grad: float32 [32, 1024, 1408], P('expert', 'dp')
- second_grad: float32 [32, 1408, 1024], P('expert', 'dp')
The draws below stay inside these ranges and needn't reach their ends.
Inputs may be any that keep to these rules, and one draw needn't show every extreme that they name: `route_ids`: each row names 4 different experts; among the 128 rows of one device no expert is named by more than 24 routes.
All inputs are finite; a program needn't handle non-finite values.
Results may differ from the reference program's by a relative error of at most 0.015.
Values may be sent and summed in bfloat16 or wider, within the bound.
A program may use at most 128 MiB of HBM per device.

```python
import math
import jax
import jax.numpy as jnp
import numpy as np
from jax import lax

D = 4096
L = 1024
H = 1408
TOPK = 4
GATE_DEN = 256
TOK_DEV = 128
EXPERTS = 32
CAP = 24
TOKENS = 32768
N_DP = 8
N_EXPERT = 32


def with_ends(result, rng, least, largest):
    longest = result.shape.index(max(result.shape))
    spots = []
    for shift in (0, 1):
        where = [jax.random.randint(jax.random.fold_in(rng, axis), (), 0, length) for axis, length in enumerate(result.shape)]
        where[longest] = (where[longest] + shift) % result.shape[longest]
        spots.append(tuple(where))
    return result.at[spots[0]].set(least).at[spots[1]].set(largest)


def block_scale(key, shape, split, smallest, largest):
    factor_of, own = 1.0, jax.random.fold_in(key, 6)
    for dim, blocks in split:
        draws = jnp.exp(jax.random.uniform(jax.random.fold_in(own, dim), (blocks,), jnp.float32, smallest / len(split), largest / len(split)))
        factor_of = factor_of * jnp.repeat(draws, shape[dim] // blocks).reshape([-1 if axis == dim else 1 for axis in range(len(shape))])
    return factor_of


def assign_block(key, own, number, rows, amount, top, most, lean):
    ranking = jax.random.permutation(key, amount)
    heavy_load, common = load_shares(amount, rows * top, most, lean, True), load_shares(amount, rows * top, most, lean, False)
    places = jnp.arange(amount)

    def named(tallies, offset_by):
        used = int((tallies > 0).sum())
        fixed = max(1, used // 4)
        passed = fixed + (places - fixed + offset_by * (used - fixed)) % max(1, amount - fixed)
        return jnp.zeros((amount,), jnp.int32).at[ranking[jnp.where(places < fixed, places, passed)]].set(jnp.asarray(tallies, jnp.int32))

    tallies = jnp.where(number % 4 == 0, named(heavy_load, number // 4), named(common, number - number // 4 - 1))
    mixed = jax.random.permutation(jax.random.fold_in(own, 3), amount)
    giver, taker = mixed[0:amount // 2 * 2:2], mixed[1:amount // 2 * 2:2]
    slack = jnp.minimum(tallies[giver] - 1, most - tallies[taker]) // 2
    slack = jnp.where((giver == ranking[0]) | (taker == ranking[0]) | (tallies[taker] == 0), 0, jnp.maximum(slack, 0))
    passed = jax.random.randint(jax.random.fold_in(own, 4), (amount // 2,), 0, 1 << 20) % (slack + 1)
    tallies = tallies.at[giver].add(-passed).at[taker].add(passed)
    items = jnp.searchsorted(jnp.cumsum(tallies), jnp.arange(rows * top), side="right").astype(jnp.int32)
    table = items.reshape(top, rows).T
    table = table[jax.random.permutation(jax.random.fold_in(own, 1), rows)]
    offset_by = jax.random.randint(jax.random.fold_in(own, 2), (rows, 1), 0, top)
    return jnp.take_along_axis(table, (jnp.arange(top)[None, :] + offset_by) % top, axis=1)


def load_shares(amount, total, reach, slope, full):
    weights = [(1 << 20) // math.isqrt(grade ** slope) + 1 for grade in range(1, amount + 1)]
    largest = reach if full else min(reach, max(-(-total // amount), total * weights[0] // sum(weights)))
    least = 1 if total - largest >= amount - 1 else 0
    counts, surplus = [largest] + [least] * (amount - 1), total - largest - least * (amount - 1)
    while surplus > 0:
        free = [i for i in range(1, amount) if counts[i] < largest] or [i for i in range(1, amount) if counts[i] < reach]
        mass, left = sum([weights[i] for i in free]), surplus
        for i in free:
            extra = min(reach - counts[i], max(1, left * weights[i] // mass), surplus)
            counts[i] = counts[i] + extra
            surplus = surplus - extra
    return np.array(counts)


def normal_values(own_key, dims, width, reach, cuts=(), held_as=jnp.bfloat16):
    level = block_scale(own_key, dims, cuts, -0.22, 0.18) if cuts else 1.0
    values = jax.random.normal(own_key, dims, jnp.float32) * width * level
    return jnp.minimum(jnp.maximum(values, -reach), reach).astype(held_as)


def setup_inputs(seed: int = 0) -> dict:
    splits = jax.random.split(jax.random.key(seed), 8)
    tokens = normal_values(splits[0], (TOKENS, D), 1.0, 6.0, ((0, 256),))
    latent_proj = normal_values(splits[1], (D, L), D ** -0.5, 0.09375, ((0, 256),))
    first_weight = normal_values(splits[2], (EXPERTS, L, H), L ** -0.5, 0.1875, ((0, 32), (1, 8)))
    second_weight = normal_values(splits[3], (EXPERTS, H, L), H ** -0.5, 0.15625, ((0, 32), (1, 8)))
    route_ids_keys = jax.random.split(jax.random.fold_in(splits[4], 1), TOKENS // TOK_DEV)
    route_ids_turns = jax.random.permutation(jax.random.fold_in(splits[4], 3), TOKENS // TOK_DEV)
    route_ids = jax.vmap(lambda own, number: assign_block(jax.random.fold_in(splits[4], 2), own, number, TOK_DEV, EXPERTS, TOPK, CAP, 2))(route_ids_keys, route_ids_turns).reshape((TOKENS, TOPK))
    gate_numer = with_ends(jax.random.randint(splits[5], (TOKENS, TOPK), 1, GATE_DEN + 1), jax.random.fold_in(splits[5], 1), 1, GATE_DEN).astype(jnp.int32)
    out_cotangent = normal_values(splits[6], (TOKENS, L), 1.0, 6.0, ((0, 256),))
    return dict(tokens=tokens, latent_proj=latent_proj, first_weight=first_weight, second_weight=second_weight, route_ids=route_ids, gate_numer=gate_numer, out_cotangent=out_cotangent)


def reference(tokens, latent_proj, first_weight, second_weight, route_ids, gate_numer, out_cotangent):
    latent = jnp.dot(tokens, latent_proj, preferred_element_type=jnp.float32).astype(jnp.bfloat16)
    group_tokens = N_EXPERT * TOK_DEV
    group_slots = N_EXPERT * CAP
    group_routes = group_tokens * TOPK
    blank = jnp.zeros((1, L), jnp.bfloat16)
    latent_groups = latent.reshape(N_DP, group_tokens, L)
    cot_groups = out_cotangent.reshape(N_DP, group_tokens, L)
    id_groups = route_ids.reshape(N_DP, group_routes)
    gate_groups = (gate_numer.astype(jnp.float32) / GATE_DEN).reshape(N_DP, group_routes)

    def per_expert(total, expert):
        first_mat = first_weight[expert]
        second_mat = second_weight[expert]

        def per_group(inner, group):
            acc_total, first_sum, second_sum = inner
            marks = id_groups[group] == expert
            chosen = jnp.nonzero(marks, size=group_slots, fill_value=group_routes)[0].astype(jnp.int32)
            owner = (chosen // TOPK).astype(jnp.int32)
            lat_rows = jnp.concatenate([latent_groups[group], blank])[owner]
            weights = jnp.concatenate([gate_groups[group], jnp.zeros((1,), jnp.float32)])[chosen]
            cot_rows = jnp.concatenate([cot_groups[group], blank])[owner].astype(jnp.float32)
            routed = (weights[:, None] * cot_rows).astype(jnp.bfloat16)
            preact = jnp.dot(lat_rows, first_mat, preferred_element_type=jnp.float32)
            active = jnp.maximum(preact, 0.0)
            hidden = (active * active).astype(jnp.bfloat16)
            grad_hidden = jnp.dot(routed, second_mat.T, preferred_element_type=jnp.float32)
            grad_preact = (grad_hidden * 2.0 * active).astype(jnp.bfloat16)
            route_grad = jnp.dot(grad_preact, first_mat.T, preferred_element_type=jnp.float32).astype(jnp.bfloat16)
            first_part = jnp.dot(lat_rows.T, grad_preact, preferred_element_type=jnp.float32).astype(jnp.bfloat16)
            second_part = jnp.dot(hidden.T, routed, preferred_element_type=jnp.float32).astype(jnp.bfloat16)
            first_part = lax.optimization_barrier(first_part).astype(jnp.float32)
            second_part = lax.optimization_barrier(second_part).astype(jnp.float32)
            target = jnp.where(owner < group_tokens, group * group_tokens + owner, TOKENS).astype(jnp.int32)
            acc_total = acc_total.at[target].add(route_grad.astype(jnp.float32))
            return (acc_total, first_sum + first_part, second_sum + second_part), None

        start = (total, jnp.zeros((L, H), jnp.float32), jnp.zeros((H, L), jnp.float32))
        (total, first_sum, second_sum), unused = lax.scan(per_group, start, jnp.arange(N_DP, dtype=jnp.int32))
        return total, (first_sum, second_sum)

    total = jnp.zeros((TOKENS + 1, L), jnp.float32)
    total, (first_grad, second_grad) = lax.scan(per_expert, total, jnp.arange(EXPERTS, dtype=jnp.int32))
    grad_latent = total[:TOKENS].astype(jnp.bfloat16)
    grad_tokens = jnp.dot(grad_latent, latent_proj.T, preferred_element_type=jnp.float32).astype(jnp.bfloat16)
    return grad_tokens, first_grad, second_grad
```

```python
import jax
import jax.numpy as jnp
from jax import lax
from jax.experimental import pallas as pl
from jax.experimental.pallas import tpu as pltpu
from jax.sharding import PartitionSpec as P

GATE_DEN = 256
MESH = pl.DeviceIdType.MESH
BF = jnp.bfloat16
F32 = jnp.float32
NZ = 8
NX = 4
NE = 32
CAP = 24
SLOTS = NE * CAP


def contract_last(left, right):
    return lax.dot_general(
        left, right, (((1,), (1,)), ((), ())), preferred_element_type=jnp.float32
    )


def contract_first(left, right):
    return lax.dot_general(
        left, right, (((0,), (0,)), ((), ())), preferred_element_type=jnp.float32
    )


def enter(d, e):
    barrier = pltpu.get_barrier_semaphore()

    def greet_plane(i, carry):
        pl.semaphore_signal(
            barrier, inc=1, device_id=(d, lax.rem(e + i, NE)), device_id_type=MESH
        )
        return carry

    def greet_column(i, carry):
        pl.semaphore_signal(
            barrier, inc=1, device_id=(lax.rem(d + i, NZ), e), device_id_type=MESH
        )
        return carry

    lax.fori_loop(1, NE, greet_plane, 0)
    lax.fori_loop(1, NZ, greet_column, 0)
    pl.semaphore_wait(barrier, NE - 1 + NZ - 1)


def gather_kernel(
    tokens_ref,
    proj_ref,
    w1_ref,
    w2_ref,
    ids_ref,
    gate_ref,
    cot_ref,
    full_ref,
    w1_out,
    w2_out,
    lat_out,
    cot_out,
    col,
    pick,
    acc,
    send_lat,
    send_cot,
    barrier_free,
    zp_send,
    zp_recv,
    wz_send,
    wz_recv,
    ax_send,
    ax_recv,
    mate_send,
    mate_recv,
    lat_send_sem,
    lat_recv_sem,
    cot_send_sem,
    cot_recv_sem,
    local_sem,
):
    d = lax.axis_index("dp")
    e = lax.axis_index("expert")
    x, y, c = e // 8, (e // 2) % NX, e % 2
    mate = (x * NX + y) * 2 + (1 - c)
    pending = []

    def remote(src, dst, ssem, rsem, dev):
        copy = pltpu.make_async_remote_copy(
            src_ref=src, dst_ref=dst, send_sem=ssem, recv_sem=rsem, device_id=dev, device_id_type=MESH
        )
        copy.start()
        pending.append(copy)
        return copy

    def arrived(dst, rsem):
        pltpu.make_async_remote_copy(
            src_ref=dst, dst_ref=dst, send_sem=rsem, recv_sem=rsem, device_id=(d, e), device_id_type=MESH
        ).wait_recv()

    enter(d, e)

    for i in range(1, NZ):
        remote(proj_ref, col.at[d, e], zp_send.at[i], zp_recv.at[i], (lax.rem(d + i, NZ), e))
    own = [pltpu.make_async_copy(proj_ref, col.at[d, e], local_sem.at[0])]
    own[0].start()

    weights = ((w1_ref, w1_out, 128), (w2_ref, w2_out, 176))
    for k, (src, dst, rows) in enumerate(weights):
        copy = pltpu.make_async_copy(src.at[0], dst.at[d], local_sem.at[1 + k])
        copy.start()
        own.append(copy)
    right, left = lax.rem(d + 1, NZ), lax.rem(d + NZ - 1, NZ)

    def halves(k, way):
        rows = weights[k][2]
        cut = 64 if k == 0 else 96
        return pl.ds(0, cut) if way == 0 else pl.ds(cut, rows - cut)

    def ring_send(s, k, way):
        src, dst, rows = weights[k]
        owner = lax.rem(d - s + NZ, NZ) if way == 0 else lax.rem(d + s, NZ)
        to = (right, e) if way == 0 else (left, e)
        part = halves(k, way) if s == 3 else pl.ds(0, rows)
        source = src.at[0] if s == 0 else dst.at[owner, part]
        remote(source, dst.at[owner, part], wz_send.at[s, k, way], wz_recv.at[s, k, way], to)

    def ring_step(s, k):
        dst, rows = weights[k][1:]
        for way in (0, 1):
            owner = lax.rem(d - s - 1 + NZ, NZ) if way == 0 else lax.rem(d + s + 1, NZ)
            part = halves(k, way) if s == 3 else pl.ds(0, rows)
            arrived(dst.at[owner, part], wz_recv.at[s, k, way])
            if s < 3:
                ring_send(s + 1, k, way)

    for k in (0, 1):
        for way in (0, 1):
            ring_send(0, k, way)

    slot = lax.broadcasted_iota(jnp.int32, (SLOTS, 128), 0)
    of_expert = (slot * 2731) >> 16
    rank_in = (slot - of_expert * CAP).astype(F32)
    named = jnp.zeros((SLOTS, 128), F32)
    gates = jnp.zeros((SLOTS, 128), F32)
    for k in range(4):
        hit = ids_ref[k : k + 1, :] == of_expert
        named = jnp.where(hit, 1.0, named)
        gates = jnp.where(hit, gate_ref[k : k + 1, :].astype(F32) * (1.0 / GATE_DEN), gates)
    before = lax.broadcasted_iota(jnp.int32, (128, 128), 0) < lax.broadcasted_iota(
        jnp.int32, (128, 128), 1
    )
    rank = jnp.dot(named.astype(BF), jnp.where(before, 1.0, 0.0).astype(BF), preferred_element_type=F32)
    chosen = jnp.logical_and(named > 0.0, rank == rank_in)
    pick[0] = jnp.where(chosen, 1.0, 0.0).astype(BF)
    pick[1] = jnp.where(chosen, gates, 0.0).astype(BF)

    def pack(which, rows_ref, out):
        for j in range(4):
            block = jnp.dot(
                pick[which, 192 * j : 192 * (j + 1), :], rows_ref[...], preferred_element_type=F32
            )
            for i in range(8):
                out[8 * j + i] = block[CAP * i : CAP * (i + 1), :].astype(BF)

    pack(1, cot_ref, send_cot)

    for i in range(1, NZ):
        arrived(col.at[lax.rem(d - i + NZ, NZ), e], zp_recv.at[i])
    own[0].wait()

    pos = ((x, y), (y, x))

    def device(h, p, q):
        p, q = lax.rem(p + 2 * NX, NX), lax.rem(q + 2 * NX, NX)
        return (p * NX + q) * 2 + c if h == 0 else (q * NX + p) * 2 + c

    def piece(h, who, sub=None):
        if sub is None:
            return col.at[pl.ds(4 * h, 4), who]
        return col.at[pl.ds(4 * h + 2 * sub, 2), who]

    def share(h, who, n):
        remote(piece(h, who), piece(h, who), mate_send.at[h, n], mate_recv.at[h, n], (d, mate))

    def spread(h, axis, who, n, sub=None, way=None):
        p, q = pos[h]
        for w in (0, 1) if way is None else (way,):
            step = 1 - 2 * w
            to = device(h, p + step, q) if axis == 0 else device(h, p, q + step)
            m = w if sub is None else 2 + w
            remote(
                piece(h, who, sub),
                piece(h, who, sub),
                ax_send.at[h, n, m],
                ax_recv.at[h, n, m],
                (d, to),
            )

    for h in (0, 1):
        p, q = pos[h]
        spread(h, 0, device(h, p, q), 0)
    for h in (0, 1):
        p, q = pos[h]
        spread(h, 1, device(h, p, q), 1)
        share(h, device(h, p, q), 0)
    for h in (0, 1):
        p, q = pos[h]
        for w in (0, 1):
            who = device(h, p - 1 + 2 * w, q)
            arrived(piece(h, who), ax_recv.at[h, 0, w])
            spread(h, 0, who, 0, sub=w, way=w)
            spread(h, 1, who, 2 + w)
            share(h, who, 1 + w)
    for h in (0, 1):
        p, q = pos[h]
        who = device(h, p + 2, q)
        for w in (0, 1):
            arrived(piece(h, who, w), ax_recv.at[h, 0, 2 + w])
        spread(h, 1, who, 4)
        share(h, who, 3)
    ring_step(0, 0)

    def second_stage(n):
        for h in (0, 1):
            p, q = pos[h]
            r = p + (0, -1, 1, 2)[n]
            for w in (0, 1):
                who = device(h, r, q - 1 + 2 * w)
                arrived(piece(h, who), ax_recv.at[h, 1 + n, w])
                spread(h, 1, who, 1 + n, sub=w, way=w)
                share(h, who, 4 + 3 * n + w)

    def second_stage_far(n):
        for h in (0, 1):
            p, q = pos[h]
            r = p + (0, -1, 1, 2)[n]
            who = device(h, r, q + 2)
            for w in (0, 1):
                arrived(piece(h, who, w), ax_recv.at[h, 1 + n, 2 + w])
            share(h, who, 6 + 3 * n)

    second_stage(0)
    second_stage(1)
    second_stage(2)
    ring_step(0, 1)
    second_stage(3)

    def dispatch(buf, out, ssem, rsem):
        def go(i, carry):
            to = lax.rem(e + i, NE)
            pltpu.make_async_remote_copy(
                src_ref=buf.at[to],
                dst_ref=out.at[e],
                send_sem=ssem.at[i],
                recv_sem=rsem.at[i],
                device_id=(d, to),
                device_id_type=MESH,
            ).start()
            return carry

        lax.fori_loop(1, NE, go, 0)
        copy = pltpu.make_async_copy(buf.at[e], out.at[e], rsem.at[0])
        copy.start()

    def landed(buf, out, ssem, rsem):
        def go(i, carry):
            copy = pltpu.make_async_remote_copy(
                src_ref=buf.at[lax.rem(e + i, NE)],
                dst_ref=out.at[lax.rem(e - i + NE, NE)],
                send_sem=ssem.at[i],
                recv_sem=rsem.at[i],
                device_id=(d, lax.rem(e + i, NE)),
                device_id_type=MESH,
            )
            copy.wait_send()
            copy.wait_recv()
            return carry

        lax.fori_loop(1, NE, go, 0)
        pltpu.make_async_copy(buf.at[e], out.at[e], rsem.at[0]).wait()

    dispatch(send_cot, cot_out, cot_send_sem, cot_recv_sem)
    for n in range(4):
        second_stage_far(n)
    ring_step(1, 0)

    def other(h, p, q):
        p, q = lax.rem(p + 2 * NX, NX), lax.rem(q + 2 * NX, NX)
        return ((p * NX + q) if h == 0 else (q * NX + p)) * 2 + (1 - c)

    order = [(0, 0), (-1, 0), (1, 0), (2, 0)]
    for n in range(4):
        r = (0, -1, 1, 2)[n]
        order += [(r, -1), (r, 1), (r, 2)]
    for h in (0, 1):
        p, q = pos[h]
        for n, (a, b) in enumerate(order):
            arrived(piece(h, other(h, p + a, q + b)), mate_recv.at[h, n])

    keep = pltpu.make_async_copy(col, full_ref, local_sem.at[3])
    keep.start()
    acc[...] = jnp.zeros_like(acc)

    def latent_step(j, carry):
        block = col[j].reshape(512, 1024)
        acc[...] += jnp.dot(
            tokens_ref[:, pl.ds(pl.multiple_of(j * 512, 512), 512)], block, preferred_element_type=F32
        )
        return carry

    lax.fori_loop(0, NZ, latent_step, 0)
    ring_step(1, 1)
    latent = acc[...].astype(BF)
    for j in range(4):
        block = jnp.dot(pick[0, 192 * j : 192 * (j + 1), :], latent, preferred_element_type=F32)
        for i in range(8):
            send_lat[8 * j + i] = block[CAP * i : CAP * (i + 1), :].astype(BF)
    dispatch(send_lat, lat_out, lat_send_sem, lat_recv_sem)
    ring_step(2, 0)
    ring_step(2, 1)
    landed(send_cot, cot_out, cot_send_sem, cot_recv_sem)
    landed(send_lat, lat_out, lat_send_sem, lat_recv_sem)
    ring_step(3, 0)
    ring_step(3, 1)
    for copy in pending:
        copy.wait_send()
    for copy in own[1:]:
        copy.wait()
    keep.wait()


def gather_all(tokens, proj, w1, w2, ids, gate, cot):
    anywhere = pl.BlockSpec(memory_space=pl.ANY)
    vmem = pl.BlockSpec(memory_space=pltpu.VMEM)
    dma = pltpu.SemaphoreType.DMA
    return pl.pallas_call(
        gather_kernel,
        out_shape=(
            jax.ShapeDtypeStruct((NZ, NE, 16, 1024), BF),
            jax.ShapeDtypeStruct((NZ, 128, 1408), BF),
            jax.ShapeDtypeStruct((NZ, 176, 1024), BF),
            jax.ShapeDtypeStruct((NE, CAP, 1024), BF),
            jax.ShapeDtypeStruct((NE, CAP, 1024), BF),
        ),
        in_specs=[vmem, anywhere, anywhere, anywhere, vmem, vmem, vmem],
        out_specs=(anywhere,) * 5,
        scratch_shapes=[
            pltpu.VMEM((NZ, NE, 16, 1024), BF),
            pltpu.VMEM((2, SLOTS, 128), BF),
            pltpu.VMEM((128, 1024), F32),
            pltpu.VMEM((NE, CAP, 1024), BF),
            pltpu.VMEM((NE, CAP, 1024), BF),
            pltpu.SemaphoreType.REGULAR,
            dma((NZ,)),
            dma((NZ,)),
            dma((4, 2, 2)),
            dma((4, 2, 2)),
            dma((2, 5, 4)),
            dma((2, 5, 4)),
            dma((2, 16)),
            dma((2, 16)),
            dma((NE,)),
            dma((NE,)),
            dma((NE,)),
            dma((NE,)),
            dma((4,)),
        ],
        compiler_params=pltpu.CompilerParams(
            collective_id=0, has_side_effects=True, vmem_limit_bytes=48 * 1024 * 1024
        ),
        name="gather_dispatch",
    )(tokens, proj, w1, w2, ids, gate, cot)


def on_device(
    tokens, latent_proj, first_weight, second_weight, route_ids, gate_numer, out_cotangent
):
    experts = lax.axis_size("expert")
    tok_count, top_count = route_ids.shape
    width = latent_proj.shape[1]
    capacity = CAP
    routes = tok_count * top_count
    slots = experts * capacity
    full, first_full, second_full, recv_latent, recv_cotangent = gather_all(
        tokens,
        latent_proj,
        first_weight,
        second_weight,
        route_ids.T,
        gate_numer.T,
        out_cotangent,
    )
    projection = full.reshape(4096, width)
    flat_ids = route_ids.reshape(routes)
    onehot = (flat_ids[:, None] == jnp.arange(experts, dtype=jnp.int32)[None, :]).astype(jnp.int32)
    position = jnp.sum((jnp.cumsum(onehot, axis=0) - 1) * onehot, axis=1)
    target = flat_ids * capacity + position
    slot_rows = recv_latent.reshape(slots, width)
    slot_cot = recv_cotangent.reshape(slots, width)
    first_mat = first_full.reshape(1024, 1408)
    second_mat = second_full.reshape(1408, 1024)
    preact = jnp.dot(slot_rows, first_mat, preferred_element_type=jnp.float32)
    active = jnp.maximum(preact, 0.0)
    grad_hidden = contract_last(slot_cot, second_mat)
    grad_preact = (grad_hidden * 2.0 * active).astype(jnp.bfloat16)
    grad_latent = contract_last(grad_preact, first_mat)
    hidden = (active * active).astype(jnp.bfloat16)
    back_rows = grad_latent.astype(jnp.bfloat16).reshape(experts, capacity, width)
    returned = lax.all_to_all(back_rows, "expert", split_axis=0, concat_axis=0, tiled=True)
    first_term = contract_first(slot_rows, grad_preact)
    second_term = contract_first(hidden, slot_cot)
    first_grad, second_grad = (
        lax.psum_scatter(
            first_term[None].astype(jnp.bfloat16), "dp", scatter_dimension=1, tiled=True
        ).astype(jnp.float32),
        lax.psum_scatter(
            second_term[None].astype(jnp.bfloat16), "dp", scatter_dimension=1, tiled=True
        ).astype(jnp.float32),
    )
    route_grad = returned.reshape(slots, width)[target].astype(jnp.float32)
    token_grad = jnp.sum(route_grad.reshape(tok_count, top_count, width), axis=1).astype(
        jnp.bfloat16
    )
    grad_tokens = contract_last(token_grad, projection).astype(jnp.bfloat16)
    return (grad_tokens, first_grad, second_grad)


def solution(mesh):
    return jax.shard_map(
        on_device,
        mesh=mesh,
        in_specs=(
            P(("dp", "expert"), None),
            P(("dp", "expert"), None),
            P("expert", "dp", None),
            P("expert", "dp", None),
            P(("dp", "expert"), None),
            P(("dp", "expert"), None),
            P(("dp", "expert"), None),
        ),
        out_specs=(P(("dp", "expert"), None), P("expert", "dp", None), P("expert", "dp", None)),
        check_vma=False,
    )
```

```python
import jax
import jax.numpy as jnp
from jax import lax
from jax.experimental import pallas as pl
from jax.experimental.pallas import tpu as pltpu
from jax.sharding import PartitionSpec as P

GATE_DEN = 256
MESH = pl.DeviceIdType.MESH
BF = jnp.bfloat16
F32 = jnp.float32
NZ = 8
NX = 4
NE = 32
CAP = 24
SLOTS = NE * CAP


def contract_last(left, right):
    return lax.dot_general(
        left, right, (((1,), (1,)), ((), ())), preferred_element_type=jnp.float32
    )


def enter(d, e):
    barrier = pltpu.get_barrier_semaphore()

    def greet_plane(i, carry):
        pl.semaphore_signal(
            barrier, inc=1, device_id=(d, lax.rem(e + i, NE)), device_id_type=MESH
        )
        return carry

    def greet_column(i, carry):
        pl.semaphore_signal(
            barrier, inc=1, device_id=(lax.rem(d + i, NZ), e), device_id_type=MESH
        )
        return carry

    lax.fori_loop(1, NE, greet_plane, 0)
    lax.fori_loop(1, NZ, greet_column, 0)
    pl.semaphore_wait(barrier, NE - 1 + NZ - 1)


def layer_kernel(
    tokens_in,
    proj_ref,
    w1_ref,
    w2_ref,
    ids_ref,
    gate_ref,
    cot_in,
    gt_out,
    g1_out,
    g2_out,
    col,
    w1_out,
    w2_out,
    lat_out,
    cot_out,
    tokens_ref,
    cot_ref,
    pick,
    back_pick,
    acc,
    send_lat,
    send_cot,
    rows,
    rows_t,
    cots,
    hidden_t,
    grad_pre,
    back_send,
    back_recv,
    back_rows,
    sum1_send,
    sum1_recv,
    sum2_send,
    sum2_recv,
    gt_stage,
    g1_stage,
    g2_stage,
    zp_send,
    zp_recv,
    wz_send,
    wz_recv,
    ax_send,
    ax_recv,
    mate_send,
    mate_recv,
    lat_send_sem,
    lat_recv_sem,
    cot_send_sem,
    cot_recv_sem,
    back_send_sem,
    back_recv_sem,
    sum_send,
    sum_recv,
    local_sem,
):
    d = lax.axis_index("dp")
    e = lax.axis_index("expert")
    x, y, c = e // 8, (e // 2) % NX, e % 2
    mate = (x * NX + y) * 2 + (1 - c)
    pending = []

    def remote(src, dst, ssem, rsem, dev):
        copy = pltpu.make_async_remote_copy(
            src_ref=src, dst_ref=dst, send_sem=ssem, recv_sem=rsem, device_id=dev, device_id_type=MESH
        )
        copy.start()
        pending.append(copy)
        return copy

    def arrived(dst, rsem):
        pltpu.make_async_remote_copy(
            src_ref=dst, dst_ref=dst, send_sem=rsem, recv_sem=rsem, device_id=(d, e), device_id_type=MESH
        ).wait_recv()

    fetch = [
        pltpu.make_async_copy(tokens_in, tokens_ref, local_sem.at[3]),
        pltpu.make_async_copy(cot_in, cot_ref, local_sem.at[4]),
    ]
    for copy in fetch:
        copy.start()
    enter(d, e)

    for i in range(1, NZ):
        remote(proj_ref, col.at[d, e], zp_send.at[i], zp_recv.at[i], (lax.rem(d + i, NZ), e))
    own = [pltpu.make_async_copy(proj_ref, col.at[d, e], local_sem.at[0])]
    own[0].start()

    weights = ((w1_ref, w1_out, 128), (w2_ref, w2_out, 176))
    def block_of(k, owner, first=0, count=None):
        span = weights[k][2]
        start = pl.multiple_of(owner * span + first, 16)
        return weights[k][1].at[pl.ds(start, span if count is None else count)]

    for k, (src, dst, _) in enumerate(weights):
        copy = pltpu.make_async_copy(src.at[0], block_of(k, d), local_sem.at[1 + k])
        copy.start()
        own.append(copy)
    right, left = lax.rem(d + 1, NZ), lax.rem(d + NZ - 1, NZ)

    cuts = (64, 96)

    def halves(k, way):
        return (0, cuts[k]) if way == 0 else (cuts[k], weights[k][2] - cuts[k])

    def ring_send(s, k, way):
        owner = lax.rem(d - s + NZ, NZ) if way == 0 else lax.rem(d + s, NZ)
        to = (right, e) if way == 0 else (left, e)
        part = halves(k, way) if s == 3 else (0, weights[k][2])
        target = block_of(k, owner, *part)
        source = weights[k][0].at[0] if s == 0 else target
        remote(source, target, wz_send.at[s, k, way], wz_recv.at[s, k, way], to)

    def ring_step(s, k):
        for way in (0, 1):
            owner = lax.rem(d - s - 1 + NZ, NZ) if way == 0 else lax.rem(d + s + 1, NZ)
            part = halves(k, way) if s == 3 else (0, weights[k][2])
            arrived(block_of(k, owner, *part), wz_recv.at[s, k, way])
            if s < 3:
                ring_send(s + 1, k, way)

    for k in (0, 1):
        for way in (0, 1):
            ring_send(0, k, way)

    slot = lax.broadcasted_iota(jnp.int32, (128, SLOTS), 1)
    of_expert = (slot * 2731) >> 16
    rank_in = (slot - of_expert * CAP).astype(F32)
    named = jnp.zeros((128, SLOTS), F32)
    gates = jnp.zeros((128, SLOTS), F32)
    for k in range(4):
        hit = ids_ref[:, k : k + 1] == of_expert
        named = jnp.where(hit, 1.0, named)
        gates = jnp.where(hit, gate_ref[:, k : k + 1].astype(F32) * (1.0 / GATE_DEN), gates)
    before = lax.broadcasted_iota(jnp.int32, (128, 128), 1) < lax.broadcasted_iota(
        jnp.int32, (128, 128), 0
    )
    rank = jnp.dot(jnp.where(before, 1.0, 0.0).astype(BF), named.astype(BF), preferred_element_type=F32)
    chosen = jnp.logical_and(named > 0.0, rank == rank_in)
    one_hot = jnp.where(chosen, 1.0, 0.0)
    back_pick[...] = one_hot.astype(BF)
    pick[0] = one_hot.T.astype(BF)
    pick[1] = jnp.where(chosen, gates, 0.0).T.astype(BF)
    for copy in fetch:
        copy.wait()

    def pack(which, rows_ref, out):
        for j in range(4):
            block = jnp.dot(
                pick[which, 192 * j : 192 * (j + 1), :], rows_ref[...], preferred_element_type=F32
            )
            for i in range(8):
                out[8 * j + i] = block[CAP * i : CAP * (i + 1), :].astype(BF)

    pack(1, cot_ref, send_cot)

    for i in range(1, NZ):
        arrived(col.at[lax.rem(d - i + NZ, NZ), e], zp_recv.at[i])
    own[0].wait()

    pos = ((x, y), (y, x))

    def device(h, p, q):
        p, q = lax.rem(p + 2 * NX, NX), lax.rem(q + 2 * NX, NX)
        return (p * NX + q) * 2 + c if h == 0 else (q * NX + p) * 2 + c

    def piece(h, who, sub=None):
        if sub is None:
            return col.at[pl.ds(4 * h, 4), who]
        return col.at[pl.ds(4 * h + 2 * sub, 2), who]

    def share(h, who, n):
        remote(piece(h, who), piece(h, who), mate_send.at[h, n], mate_recv.at[h, n], (d, mate))

    def spread(h, axis, who, n, sub=None, way=None):
        p, q = pos[h]
        for w in (0, 1) if way is None else (way,):
            step = 1 - 2 * w
            to = device(h, p + step, q) if axis == 0 else device(h, p, q + step)
            m = w if sub is None else 2 + w
            remote(
                piece(h, who, sub),
                piece(h, who, sub),
                ax_send.at[h, n, m],
                ax_recv.at[h, n, m],
                (d, to),
            )

    for h in (0, 1):
        p, q = pos[h]
        spread(h, 0, device(h, p, q), 0)
    for h in (0, 1):
        p, q = pos[h]
        spread(h, 1, device(h, p, q), 1)
        share(h, device(h, p, q), 0)
    for h in (0, 1):
        p, q = pos[h]
        for w in (0, 1):
            who = device(h, p - 1 + 2 * w, q)
            arrived(piece(h, who), ax_recv.at[h, 0, w])
            spread(h, 0, who, 0, sub=w, way=w)
            spread(h, 1, who, 2 + w)
            share(h, who, 1 + w)
    for h in (0, 1):
        p, q = pos[h]
        who = device(h, p + 2, q)
        for w in (0, 1):
            arrived(piece(h, who, w), ax_recv.at[h, 0, 2 + w])
        spread(h, 1, who, 4)
        share(h, who, 3)
    ring_step(0, 0)

    def second_stage(n):
        for h in (0, 1):
            p, q = pos[h]
            r = p + (0, -1, 1, 2)[n]
            for w in (0, 1):
                who = device(h, r, q - 1 + 2 * w)
                arrived(piece(h, who), ax_recv.at[h, 1 + n, w])
                spread(h, 1, who, 1 + n, sub=w, way=w)
                share(h, who, 4 + 3 * n + w)

    def second_stage_far(n):
        for h in (0, 1):
            p, q = pos[h]
            r = p + (0, -1, 1, 2)[n]
            who = device(h, r, q + 2)
            for w in (0, 1):
                arrived(piece(h, who, w), ax_recv.at[h, 1 + n, 2 + w])
            share(h, who, 6 + 3 * n)

    second_stage(0)
    second_stage(1)
    second_stage(2)
    ring_step(0, 1)
    second_stage(3)

    def dispatch(buf, out, ssem, rsem):
        def go(i, carry):
            to = lax.rem(e + i, NE)
            pltpu.make_async_remote_copy(
                src_ref=buf.at[to],
                dst_ref=out.at[e],
                send_sem=ssem.at[i],
                recv_sem=rsem.at[i],
                device_id=(d, to),
                device_id_type=MESH,
            ).start()
            return carry

        lax.fori_loop(1, NE, go, 0)
        copy = pltpu.make_async_copy(buf.at[e], out.at[e], rsem.at[0])
        copy.start()

    def landed(buf, out, ssem, rsem):
        def go(i, carry):
            copy = pltpu.make_async_remote_copy(
                src_ref=buf.at[lax.rem(e + i, NE)],
                dst_ref=out.at[lax.rem(e - i + NE, NE)],
                send_sem=ssem.at[i],
                recv_sem=rsem.at[i],
                device_id=(d, lax.rem(e + i, NE)),
                device_id_type=MESH,
            )
            copy.wait_send()
            copy.wait_recv()
            return carry

        lax.fori_loop(1, NE, go, 0)
        pltpu.make_async_copy(buf.at[e], out.at[e], rsem.at[0]).wait()

    dispatch(send_cot, cot_out, cot_send_sem, cot_recv_sem)
    for n in range(4):
        second_stage_far(n)
    ring_step(1, 0)

    def other(h, p, q):
        p, q = lax.rem(p + 2 * NX, NX), lax.rem(q + 2 * NX, NX)
        return ((p * NX + q) if h == 0 else (q * NX + p)) * 2 + (1 - c)

    order = [(0, 0), (-1, 0), (1, 0), (2, 0)]
    for n in range(4):
        r = (0, -1, 1, 2)[n]
        order += [(r, -1), (r, 1), (r, 2)]
    for h in (0, 1):
        p, q = pos[h]
        for n, (a, b) in enumerate(order):
            arrived(piece(h, other(h, p + a, q + b)), mate_recv.at[h, n])

    acc[...] = jnp.zeros_like(acc)

    def latent_step(j, carry):
        block = col[j].reshape(512, 1024)
        acc[...] += jnp.dot(
            tokens_ref[:, pl.ds(pl.multiple_of(j * 512, 512), 512)], block, preferred_element_type=F32
        )
        return carry

    lax.fori_loop(0, NZ, latent_step, 0)
    ring_step(1, 1)
    latent = acc[...].astype(BF)
    for j in range(4):
        block = jnp.dot(pick[0, 192 * j : 192 * (j + 1), :], latent, preferred_element_type=F32)
        for i in range(8):
            send_lat[8 * j + i] = block[CAP * i : CAP * (i + 1), :].astype(BF)
    dispatch(send_lat, lat_out, lat_send_sem, lat_recv_sem)

    def repack(buf, out):
        def go(j, carry):
            pair = jnp.concatenate([buf[2 * j].astype(F32), buf[2 * j + 1].astype(F32)], axis=0)
            out[pl.ds(pl.multiple_of(j * 48, 16), 48), :] = pair.astype(BF)
            return carry

        lax.fori_loop(0, NE // 2, go, 0)

    ring_step(2, 0)
    landed(send_cot, cot_out, cot_send_sem, cot_recv_sem)
    repack(cot_out, cots)
    ring_step(2, 1)
    landed(send_lat, lat_out, lat_send_sem, lat_recv_sem)
    repack(lat_out, rows)

    def turn(j, carry):
        part = pl.ds(pl.multiple_of(j * 128, 128), 128)
        rows_t[:, part] = rows[part, :].T
        return carry

    lax.fori_loop(0, SLOTS // 128, turn, 0)
    ring_step(3, 0)
    ring_step(3, 1)
    for copy in own[1:]:
        copy.wait()

    def hidden_tile(start, width):
        part = pl.ds(pl.multiple_of(start, 128), width)
        preact = jnp.dot(rows[...], w1_out[:, part], preferred_element_type=F32)
        active = jnp.maximum(preact, 0.0)
        hidden_t[part, :] = (active * active).astype(BF).T
        grad_hidden = contract_last(cots[...], w2_out[part, :])
        grad_pre[:, part] = (grad_hidden * 2.0 * active).astype(BF)

    def hidden_loop(j, carry):
        hidden_tile(j * 256, 256)
        return carry

    lax.fori_loop(0, 5, hidden_loop, 0)
    hidden_tile(1280, 128)

    sums = (
        (sum1_send, sum1_recv, g1_stage, 128),
        (sum2_send, sum2_recv, g2_stage, 176),
    )

    def partial_of(k, owner):
        if k == 0:
            block = rows_t[pl.ds(pl.multiple_of(owner * 128, 128), 128), :]
            return jnp.dot(block, grad_pre[...], preferred_element_type=F32)
        block = hidden_t[pl.ds(pl.multiple_of(owner * 176, 16), 176), :]
        return jnp.dot(block, cots[...], preferred_element_type=F32)

    def sum_copy(s, k, way):
        out, inp, _, span = sums[k]
        first, count = halves(k, way) if s == 0 else (0, span)
        part = pl.ds(first, count)
        return pltpu.make_async_remote_copy(
            src_ref=out.at[s, way, part],
            dst_ref=inp.at[s, way, part],
            send_sem=sum_send.at[s, k, way],
            recv_sem=sum_recv.at[s, k, way],
            device_id=((right if way == 0 else left), e),
            device_id_type=MESH,
        )

    def sum_send_off(s, k, way):
        copy = sum_copy(s, k, way)
        copy.start()
        pending.append(copy)

    def sum_step(s, k):
        out, inp, stage, span = sums[k]
        if s == 0:
            block = partial_of(k, lax.rem(d + 4, NZ)).astype(BF)
            for way in (0, 1):
                first, count = halves(k, way)
                out[0, way, first : first + count, :] = block[first : first + count, :]
                sum_send_off(0, k, way)
            return
        if s == 4:
            block = partial_of(k, d)
            for way in (0, 1):
                sum_copy(3, k, way).wait_recv()
            stage[...] = block + inp[3, 0].astype(F32) + inp[3, 1].astype(F32)
            return
        for way in (0, 1):
            owner = lax.rem(d + 4 - s, NZ) if way == 0 else lax.rem(d + 4 + s, NZ)
            block = partial_of(k, owner)
            sum_copy(s - 1, k, way).wait_recv()
            if s == 1:
                first, count = halves(k, way)
                span_in = slice(first, first + count)
                out[s, way] = block.astype(BF)
                out[s, way, span_in, :] = (
                    block[span_in, :] + inp[0, way, span_in, :].astype(F32)
                ).astype(BF)
            else:
                out[s, way] = (block + inp[s - 1, way].astype(F32)).astype(BF)
            sum_send_off(s, k, way)

    sum_step(0, 1)
    sum_step(0, 0)

    def route_tile(n, carry):
        part = pl.ds(pl.multiple_of(n * 256, 256), 256)
        block = contract_last(grad_pre[...], w1_out[part, :])
        for i in range(NE):
            back_send[i, :, part] = block[CAP * i : CAP * (i + 1), :].astype(BF)
        return carry

    lax.fori_loop(0, 4, route_tile, 0)
    dispatch(back_send, back_recv, back_send_sem, back_recv_sem)
    sum_step(1, 1)
    sum_step(1, 0)
    sum_step(2, 1)
    landed(back_send, back_recv, back_send_sem, back_recv_sem)
    repack(back_recv, back_rows)
    token_grad = jnp.dot(back_pick[...], back_rows[...], preferred_element_type=F32).astype(BF)
    sum_step(2, 0)
    sum_step(3, 1)
    sum_step(3, 0)

    def token_tile(j, carry):
        block = contract_last(token_grad, col[j].reshape(512, 1024))
        gt_stage[:, pl.ds(pl.multiple_of(j * 512, 512), 512)] = block.astype(BF)
        return carry

    lax.fori_loop(0, NZ, token_tile, 0)
    leave = [pltpu.make_async_copy(gt_stage, gt_out, local_sem.at[5])]
    leave[0].start()
    sum_step(4, 1)
    leave.append(pltpu.make_async_copy(g2_stage, g2_out.at[0], local_sem.at[6]))
    leave[1].start()
    sum_step(4, 0)
    leave.append(pltpu.make_async_copy(g1_stage, g1_out.at[0], local_sem.at[7]))
    leave[2].start()
    for copy in pending:
        copy.wait_send()
    for copy in leave:
        copy.wait()


def layer(tokens, proj, w1, w2, ids, gate, cot):
    anywhere = pl.BlockSpec(memory_space=pl.ANY)
    vmem = pl.BlockSpec(memory_space=pltpu.VMEM)
    dma = pltpu.SemaphoreType.DMA
    slots = (NE, CAP, 1024)
    flat = (SLOTS, 1024)
    return pl.pallas_call(
        layer_kernel,
        out_shape=(
            jax.ShapeDtypeStruct((128, 4096), BF),
            jax.ShapeDtypeStruct((1, 128, 1408), F32),
            jax.ShapeDtypeStruct((1, 176, 1024), F32),
        ),
        in_specs=[anywhere, anywhere, anywhere, anywhere, vmem, vmem, anywhere],
        out_specs=(anywhere,) * 3,
        scratch_shapes=[
            pltpu.VMEM((NZ, NE, 16, 1024), BF),
            pltpu.VMEM((1024, 1408), BF),
            pltpu.VMEM((1408, 1024), BF),
            pltpu.VMEM(slots, BF),
            pltpu.VMEM(slots, BF),
            pltpu.VMEM((128, 4096), BF),
            pltpu.VMEM((128, 1024), BF),
            pltpu.VMEM((2, SLOTS, 128), BF),
            pltpu.VMEM((128, SLOTS), BF),
            pltpu.VMEM((128, 1024), F32),
            pltpu.VMEM(slots, BF),
            pltpu.VMEM(slots, BF),
            pltpu.VMEM(flat, BF),
            pltpu.VMEM((1024, SLOTS), BF),
            pltpu.VMEM(flat, BF),
            pltpu.VMEM((1408, SLOTS), BF),
            pltpu.VMEM((SLOTS, 1408), BF),
            pltpu.VMEM(slots, BF),
            pltpu.VMEM(slots, BF),
            pltpu.VMEM(flat, BF),
            pltpu.VMEM((4, 2, 128, 1408), BF),
            pltpu.VMEM((4, 2, 128, 1408), BF),
            pltpu.VMEM((4, 2, 176, 1024), BF),
            pltpu.VMEM((4, 2, 176, 1024), BF),
            pltpu.VMEM((128, 4096), BF),
            pltpu.VMEM((128, 1408), F32),
            pltpu.VMEM((176, 1024), F32),
            dma((NZ,)),
            dma((NZ,)),
            dma((4, 2, 2)),
            dma((4, 2, 2)),
            dma((2, 5, 4)),
            dma((2, 5, 4)),
            dma((2, 16)),
            dma((2, 16)),
            dma((NE,)),
            dma((NE,)),
            dma((NE,)),
            dma((NE,)),
            dma((NE,)),
            dma((NE,)),
            dma((4, 2, 2)),
            dma((4, 2, 2)),
            dma((8,)),
        ],
        compiler_params=pltpu.CompilerParams(
            collective_id=0, has_side_effects=True, vmem_limit_bytes=60 * 1024 * 1024
        ),
        name="moe_backward",
    )(tokens, proj, w1, w2, ids, gate, cot)


def solution(mesh):
    return jax.shard_map(
        layer,
        mesh=mesh,
        in_specs=(
            P(("dp", "expert"), None),
            P(("dp", "expert"), None),
            P("expert", "dp", None),
            P("expert", "dp", None),
            P(("dp", "expert"), None),
            P(("dp", "expert"), None),
            P(("dp", "expert"), None),
        ),
        out_specs=(P(("dp", "expert"), None), P("expert", "dp", None), P("expert", "dp", None)),
        check_vma=False,
    )
```

```python
import jax
import jax.numpy as jnp
from jax import lax
from jax.experimental import pallas as pl
from jax.experimental.pallas import tpu as pltpu
from jax.sharding import PartitionSpec as P

GATE_DEN = 256
MESH = pl.DeviceIdType.MESH
BF = jnp.bfloat16
F32 = jnp.float32
NZ = 8
NX = 4
NE = 32
CAP = 24
SLOTS = NE * CAP
FAR_FIRST = (
    (2, 2),
    (2, 1),
    (2, 3),
    (1, 2),
    (3, 2),
    (2, 0),
    (0, 2),
    (1, 1),
    (3, 3),
    (1, 3),
    (3, 1),
    (1, 0),
    (3, 0),
    (0, 1),
    (0, 3),
)
ORDER = [(a, b, core) for core in (0, 1) for a, b in FAR_FIRST] + [(0, 0, 1)]


def contract_last(left, right):
    return lax.dot_general(
        left, right, (((1,), (1,)), ((), ())), preferred_element_type=jnp.float32
    )


def contract_first(left, right):
    return lax.dot_general(
        left, right, (((0,), (0,)), ((), ())), preferred_element_type=jnp.float32
    )


def enter(d, e):
    barrier = pltpu.get_barrier_semaphore()

    def greet_plane(i, carry):
        pl.semaphore_signal(
            barrier, inc=1, device_id=(d, lax.rem(e + i, NE)), device_id_type=MESH
        )
        return carry

    def greet_column(i, carry):
        pl.semaphore_signal(
            barrier, inc=1, device_id=(lax.rem(d + i, NZ), e), device_id_type=MESH
        )
        return carry

    lax.fori_loop(1, NE, greet_plane, 0)
    lax.fori_loop(1, NZ, greet_column, 0)
    pl.semaphore_wait(barrier, NE - 1 + NZ - 1)


def layer_kernel(
    tokens_in,
    proj_ref,
    w1_ref,
    w2_ref,
    ids_ref,
    gate_ref,
    cot_in,
    gt_out,
    g1_out,
    g2_out,
    col,
    w1_out,
    w2_out,
    lat_out,
    cot_out,
    tokens_ref,
    cot_ref,
    pick,
    acc,
    send_lat,
    send_cot,
    rows,
    rows_t,
    cots,
    hidden_t,
    grad_hid,
    grad_pre,
    back_send,
    back_recv,
    back_rows,
    sum1_send,
    sum1_recv,
    sum2_send,
    sum2_recv,
    gt_stage,
    g1_stage,
    g2_stage,
    zp_send,
    zp_recv,
    wz_send,
    wz_recv,
    ax_send,
    ax_recv,
    mate_send,
    mate_recv,
    lat_send_sem,
    lat_recv_sem,
    cot_send_sem,
    cot_recv_sem,
    back_send_sem,
    back_recv_sem,
    sum_send,
    sum_recv,
    local_sem,
):
    d = lax.axis_index("dp")
    e = lax.axis_index("expert")
    x, y, c = e // 8, (e // 2) % NX, e % 2
    mate = (x * NX + y) * 2 + (1 - c)
    pending = []

    def remote(src, dst, ssem, rsem, dev):
        copy = pltpu.make_async_remote_copy(
            src_ref=src, dst_ref=dst, send_sem=ssem, recv_sem=rsem, device_id=dev, device_id_type=MESH
        )
        copy.start()
        pending.append(copy)
        return copy

    def arrived(dst, rsem):
        pltpu.make_async_remote_copy(
            src_ref=dst, dst_ref=dst, send_sem=rsem, recv_sem=rsem, device_id=(d, e), device_id_type=MESH
        ).wait_recv()

    fetch = [
        pltpu.make_async_copy(tokens_in, tokens_ref, local_sem.at[3]),
        pltpu.make_async_copy(cot_in, cot_ref, local_sem.at[4]),
    ]
    for copy in fetch:
        copy.start()
    enter(d, e)

    for i in range(1, NZ):
        remote(proj_ref, col.at[d, e], zp_send.at[i], zp_recv.at[i], (lax.rem(d + i, NZ), e))
    own = [pltpu.make_async_copy(proj_ref, col.at[d, e], local_sem.at[0])]
    own[0].start()

    weights = ((w1_ref, w1_out, 128), (w2_ref, w2_out, 176))
    def block_of(k, owner, first=0, count=None):
        span = weights[k][2]
        start = pl.multiple_of(owner * span + first, 16)
        return weights[k][1].at[pl.ds(start, span if count is None else count)]

    for k, (src, dst, _) in enumerate(weights):
        copy = pltpu.make_async_copy(src.at[0], block_of(k, d), local_sem.at[1 + k])
        copy.start()
        own.append(copy)
    right, left = lax.rem(d + 1, NZ), lax.rem(d + NZ - 1, NZ)

    cuts = (64, 96)

    def part_of(k, part):
        return (0, cuts[k]) if part == 0 else (cuts[k], weights[k][2] - cuts[k])

    def ring_send(s, k, part, way):
        owner = lax.rem(d - s + NZ, NZ) if way == 0 else lax.rem(d + s, NZ)
        to = (right, e) if way == 0 else (left, e)
        first, count = part_of(k, part)
        target = block_of(k, owner, first, count)
        source = weights[k][0].at[0, pl.ds(first, count)] if s == 0 else target
        remote(source, target, wz_send.at[s, k, part, way], wz_recv.at[s, k, part, way], to)

    def ring_first(k, part):
        for way in (0, 1):
            ring_send(0, k, part, way)

    def ring_step(s, k, part):
        for way in (0, 1):
            if s == 3 and way != part:
                continue
            owner = lax.rem(d - s - 1 + NZ, NZ) if way == 0 else lax.rem(d + s + 1, NZ)
            arrived(block_of(k, owner, *part_of(k, part)), wz_recv.at[s, k, part, way])
            if s < 2 or (s == 2 and way == part):
                ring_send(s + 1, k, part, way)

    ring_first(1, 0)

    slot = lax.broadcasted_iota(jnp.int32, (SLOTS, 128), 0)
    of_expert = (slot * 2731) >> 16
    rank_in = (slot - of_expert * CAP).astype(F32)
    named = jnp.zeros((SLOTS, 128), F32)
    gates = jnp.zeros((SLOTS, 128), F32)
    for k in range(4):
        hit = ids_ref[k : k + 1, :] == of_expert
        named = jnp.where(hit, 1.0, named)
        gates = jnp.where(hit, gate_ref[k : k + 1, :].astype(F32) * (1.0 / GATE_DEN), gates)
    before = lax.broadcasted_iota(jnp.int32, (128, 128), 0) < lax.broadcasted_iota(
        jnp.int32, (128, 128), 1
    )
    rank = jnp.dot(named.astype(BF), jnp.where(before, 1.0, 0.0).astype(BF), preferred_element_type=F32)
    chosen = jnp.logical_and(named > 0.0, rank == rank_in)
    one_hot = jnp.where(chosen, 1.0, 0.0)
    pick[0] = one_hot.astype(BF)
    pick[1] = jnp.where(chosen, gates, 0.0).astype(BF)
    for copy in fetch:
        copy.wait()
    ring_first(1, 1)

    def pack(which, rows_ref, out):
        for j in range(4):
            block = jnp.dot(
                pick[which, 192 * j : 192 * (j + 1), :], rows_ref[...], preferred_element_type=F32
            )
            for i in range(8):
                out[8 * j + i] = block[CAP * i : CAP * (i + 1), :].astype(BF)

    def away(n):
        dx, dy, dc = ORDER[n]
        core = c if dc == 0 else 1 - c
        to = (lax.rem(x + dx, NX) * NX + lax.rem(y + dy, NX)) * 2 + core
        source = (lax.rem(x - dx + NX, NX) * NX + lax.rem(y - dy + NX, NX)) * 2 + core
        return to, source

    def dispatch(buf, out, ssem, rsem, lo=0, hi=NE - 1):
        for n in range(lo, hi):
            to = away(n)[0]
            pltpu.make_async_remote_copy(
                src_ref=buf.at[to],
                dst_ref=out.at[e],
                send_sem=ssem.at[n],
                recv_sem=rsem.at[n],
                device_id=(d, to),
                device_id_type=MESH,
            ).start()
        if hi == NE - 1:
            pltpu.make_async_copy(buf.at[e], out.at[e], rsem.at[hi]).start()

    def landed(buf, out, ssem, rsem):
        for n in range(NE - 1):
            to, source = away(n)
            copy = pltpu.make_async_remote_copy(
                src_ref=buf.at[to],
                dst_ref=out.at[source],
                send_sem=ssem.at[n],
                recv_sem=rsem.at[n],
                device_id=(d, to),
                device_id_type=MESH,
            )
            copy.wait_send()
            copy.wait_recv()
        pltpu.make_async_copy(buf.at[e], out.at[e], rsem.at[NE - 1]).wait()

    pack(1, cot_ref, send_cot)
    ring_first(0, 0)
    dispatch(send_cot, cot_out, cot_send_sem, cot_recv_sem, 0, 15)
    ring_first(0, 1)

    for i in range(1, NZ):
        arrived(col.at[lax.rem(d - i + NZ, NZ), e], zp_recv.at[i])
    own[0].wait()

    pos = ((x, y), (y, x))

    def device(h, p, q):
        p, q = lax.rem(p + 2 * NX, NX), lax.rem(q + 2 * NX, NX)
        return (p * NX + q) * 2 + c if h == 0 else (q * NX + p) * 2 + c

    def piece(h, who, sub=None):
        if sub is None:
            return col.at[pl.ds(4 * h, 4), who]
        return col.at[pl.ds(4 * h + 2 * sub, 2), who]

    def share(h, who, n):
        remote(piece(h, who), piece(h, who), mate_send.at[h, n], mate_recv.at[h, n], (d, mate))

    def spread(h, axis, who, n, sub=None, way=None):
        p, q = pos[h]
        for w in (0, 1) if way is None else (way,):
            step = 1 - 2 * w
            to = device(h, p + step, q) if axis == 0 else device(h, p, q + step)
            m = w if sub is None else 2 + w
            remote(
                piece(h, who, sub),
                piece(h, who, sub),
                ax_send.at[h, n, m],
                ax_recv.at[h, n, m],
                (d, to),
            )

    for h in (0, 1):
        p, q = pos[h]
        spread(h, 0, device(h, p, q), 0)
    for h in (0, 1):
        p, q = pos[h]
        spread(h, 1, device(h, p, q), 1)
        share(h, device(h, p, q), 0)
    ring_step(0, 1, 0)
    for h in (0, 1):
        p, q = pos[h]
        for w in (0, 1):
            who = device(h, p - 1 + 2 * w, q)
            arrived(piece(h, who), ax_recv.at[h, 0, w])
            spread(h, 0, who, 0, sub=w, way=w)
            spread(h, 1, who, 2 + w)
            share(h, who, 1 + w)
    ring_step(0, 1, 1)
    for h in (0, 1):
        p, q = pos[h]
        who = device(h, p + 2, q)
        for w in (0, 1):
            arrived(piece(h, who, w), ax_recv.at[h, 0, 2 + w])
        spread(h, 1, who, 4)
        share(h, who, 3)
    ring_step(0, 0, 0)

    def second_stage(n):
        for h in (0, 1):
            p, q = pos[h]
            r = p + (0, -1, 1, 2)[n]
            for w in (0, 1):
                who = device(h, r, q - 1 + 2 * w)
                arrived(piece(h, who), ax_recv.at[h, 1 + n, w])
                spread(h, 1, who, 1 + n, sub=w, way=w)
                share(h, who, 4 + 3 * n + w)

    def second_stage_far(n):
        for h in (0, 1):
            p, q = pos[h]
            r = p + (0, -1, 1, 2)[n]
            who = device(h, r, q + 2)
            for w in (0, 1):
                arrived(piece(h, who, w), ax_recv.at[h, 1 + n, 2 + w])
            share(h, who, 6 + 3 * n)

    second_stage(0)
    ring_step(0, 0, 1)
    second_stage(1)
    second_stage(2)
    ring_step(1, 1, 0)
    dispatch(send_cot, cot_out, cot_send_sem, cot_recv_sem, 15)
    second_stage(3)
    ring_step(1, 1, 1)

    for n in range(4):
        second_stage_far(n)
    ring_step(1, 0, 0)

    def other(h, p, q):
        p, q = lax.rem(p + 2 * NX, NX), lax.rem(q + 2 * NX, NX)
        return ((p * NX + q) if h == 0 else (q * NX + p)) * 2 + (1 - c)

    order = [(0, 0), (-1, 0), (1, 0), (2, 0)]
    for n in range(4):
        r = (0, -1, 1, 2)[n]
        order += [(r, -1), (r, 1), (r, 2)]
    for h in (0, 1):
        p, q = pos[h]
        for n, (a, b) in enumerate(order):
            arrived(piece(h, other(h, p + a, q + b)), mate_recv.at[h, n])

    acc[...] = jnp.zeros_like(acc)

    def latent_step(j, carry):
        block = col[j].reshape(512, 1024)
        acc[...] += jnp.dot(
            tokens_ref[:, pl.ds(pl.multiple_of(j * 512, 512), 512)], block, preferred_element_type=F32
        )
        return carry

    lax.fori_loop(0, NZ, latent_step, 0)
    ring_step(1, 0, 1)
    latent = acc[...].astype(BF)
    for j in range(4):
        block = jnp.dot(pick[0, 192 * j : 192 * (j + 1), :], latent, preferred_element_type=F32)
        for i in range(8):
            send_lat[8 * j + i] = block[CAP * i : CAP * (i + 1), :].astype(BF)
    dispatch(send_lat, lat_out, lat_send_sem, lat_recv_sem)

    def repack(buf, out):
        def go(j, carry):
            pair = jnp.concatenate([buf[2 * j].astype(F32), buf[2 * j + 1].astype(F32)], axis=0)
            out[pl.ds(pl.multiple_of(j * 48, 16), 48), :] = pair.astype(BF)
            return carry

        lax.fori_loop(0, NE // 2, go, 0)

    ring_step(2, 1, 0)
    ring_step(2, 1, 1)
    landed(send_cot, cot_out, cot_send_sem, cot_recv_sem)
    ring_step(2, 0, 0)
    repack(cot_out, cots)
    ring_step(2, 0, 1)
    ring_step(3, 1, 0)
    ring_step(3, 1, 1)
    own[2].wait()

    def tiles(tile):
        def go(j, carry):
            tile(j * 256, 256)
            return carry

        lax.fori_loop(0, 5, go, 0)
        tile(1280, 128)

    def cot_tile(start, width):
        part = pl.ds(pl.multiple_of(start, 128), width)
        grad_hid[:, part] = contract_last(cots[...], w2_out[part, :])

    tiles(cot_tile)
    ring_step(3, 0, 0)
    ring_step(3, 0, 1)
    own[1].wait()
    landed(send_lat, lat_out, lat_send_sem, lat_recv_sem)
    repack(lat_out, rows)

    def hidden_tile(start, width):
        part = pl.ds(pl.multiple_of(start, 128), width)
        preact = jnp.dot(rows[...], w1_out[:, part], preferred_element_type=F32)
        active = jnp.maximum(preact, 0.0)
        hidden_t[part, :] = (active * active).astype(BF).T
        grad_pre[:, part] = (grad_hid[:, part] * 2.0 * active).astype(BF)

    tiles(hidden_tile)

    def turn(j, carry):
        part = pl.ds(pl.multiple_of(j * 128, 128), 128)
        rows_t[:, part] = rows[part, :].T
        return carry

    sums = (
        (sum1_send, sum1_recv, g1_stage, 128),
        (sum2_send, sum2_recv, g2_stage, 176),
    )

    def partial_of(k, owner):
        if k == 0:
            block = rows_t[pl.ds(pl.multiple_of(owner * 128, 128), 128), :]
            return jnp.dot(block, grad_pre[...], preferred_element_type=F32)
        block = hidden_t[pl.ds(pl.multiple_of(owner * 176, 16), 176), :]
        return jnp.dot(block, cots[...], preferred_element_type=F32)

    def sum_copy(s, k, part, way):
        out, inp = sums[k][:2]
        first, count = part_of(k, part)
        span = pl.ds(first, count)
        return pltpu.make_async_remote_copy(
            src_ref=out.at[s, way, span],
            dst_ref=inp.at[s, way, span],
            send_sem=sum_send.at[s, k, part, way],
            recv_sem=sum_recv.at[s, k, part, way],
            device_id=((right if way == 0 else left), e),
            device_id_type=MESH,
        )

    def sum_send_off(s, k, part, way):
        copy = sum_copy(s, k, part, way)
        copy.start()
        pending.append(copy)

    def sum_step(s, k):
        out, inp, stage, _ = sums[k]
        if s == 0:
            block = partial_of(k, lax.rem(d + 4, NZ)).astype(BF)
            for way in (0, 1):
                first, count = part_of(k, way)
                out[0, way, first : first + count, :] = block[first : first + count, :]
                sum_send_off(0, k, way, way)
            return
        if s == 4:
            block = partial_of(k, d)
            for part in (0, 1):
                first, count = part_of(k, part)
                span = slice(first, first + count)
                for way in (0, 1):
                    sum_copy(3, k, part, way).wait_recv()
                stage[span, :] = (
                    block[span, :] + inp[3, 0, span, :].astype(F32) + inp[3, 1, span, :].astype(F32)
                )
            return
        blocks = [
            partial_of(k, lax.rem(d + 4 - s, NZ) if way == 0 else lax.rem(d + 4 + s, NZ))
            for way in (0, 1)
        ]
        for n in (0, 1):
            for way in (0, 1):
                part = 1 - way if n == 0 else way
                first, count = part_of(k, part)
                span = slice(first, first + count)
                value = blocks[way][span, :]
                if s > 1 or n == 1:
                    sum_copy(s - 1, k, part, way).wait_recv()
                    value = value + inp[s - 1, way, span, :].astype(F32)
                out[s, way, span, :] = value.astype(BF)
                sum_send_off(s, k, part, way)

    sum_step(0, 1)
    lax.fori_loop(0, SLOTS // 128, turn, 0)
    sum_step(0, 0)

    def route_tile(n, carry):
        part = pl.ds(pl.multiple_of(n * 256, 256), 256)
        block = contract_last(grad_pre[...], w1_out[part, :])
        for i in range(NE):
            back_send[i, :, part] = block[CAP * i : CAP * (i + 1), :].astype(BF)
        return carry

    lax.fori_loop(0, 4, route_tile, 0)
    dispatch(back_send, back_recv, back_send_sem, back_recv_sem)
    sum_step(1, 1)
    sum_step(1, 0)
    sum_step(2, 1)
    landed(back_send, back_recv, back_send_sem, back_recv_sem)
    repack(back_recv, back_rows)
    token_grad = contract_first(pick[0], back_rows[...]).astype(BF)
    sum_step(2, 0)
    sum_step(3, 1)
    sum_step(3, 0)

    def token_tile(j, carry):
        block = contract_last(token_grad, col[j].reshape(512, 1024))
        gt_stage[:, pl.ds(pl.multiple_of(j * 512, 512), 512)] = block.astype(BF)
        return carry

    lax.fori_loop(0, NZ, token_tile, 0)
    leave = [pltpu.make_async_copy(gt_stage, gt_out, local_sem.at[5])]
    leave[0].start()
    sum_step(4, 1)
    leave.append(pltpu.make_async_copy(g2_stage, g2_out.at[0], local_sem.at[6]))
    leave[1].start()
    sum_step(4, 0)
    leave.append(pltpu.make_async_copy(g1_stage, g1_out.at[0], local_sem.at[7]))
    leave[2].start()
    for copy in pending:
        copy.wait_send()
    for copy in leave:
        copy.wait()


def layer(tokens, proj, w1, w2, ids, gate, cot):
    anywhere = pl.BlockSpec(memory_space=pl.ANY)
    vmem = pl.BlockSpec(memory_space=pltpu.VMEM)
    dma = pltpu.SemaphoreType.DMA
    slots = (NE, CAP, 1024)
    flat = (SLOTS, 1024)
    results = pl.pallas_call(
        layer_kernel,
        out_shape=(
            jax.ShapeDtypeStruct((128, 4096), BF),
            jax.ShapeDtypeStruct((1, 128, 1408), F32),
            jax.ShapeDtypeStruct((1, 176, 1024), F32),
        ),
        in_specs=[anywhere, anywhere, anywhere, anywhere, vmem, vmem, anywhere],
        out_specs=(anywhere,) * 3,
        scratch_shapes=[
            pltpu.VMEM((NZ, NE, 16, 1024), BF),
            pltpu.VMEM((1024, 1408), BF),
            pltpu.VMEM((1408, 1024), BF),
            pltpu.VMEM(slots, BF),
            pltpu.VMEM(slots, BF),
            pltpu.VMEM((128, 4096), BF),
            pltpu.VMEM((128, 1024), BF),
            pltpu.VMEM((2, SLOTS, 128), BF),
            pltpu.VMEM((128, 1024), F32),
            pltpu.VMEM(slots, BF),
            pltpu.VMEM(slots, BF),
            pltpu.VMEM(flat, BF),
            pltpu.VMEM((1024, SLOTS), BF),
            pltpu.VMEM(flat, BF),
            pltpu.VMEM((1408, SLOTS), BF),
            pltpu.VMEM((SLOTS, 1408), F32),
            pltpu.VMEM((SLOTS, 1408), BF),
            pltpu.VMEM(slots, BF),
            pltpu.VMEM(slots, BF),
            pltpu.VMEM(flat, BF),
            pltpu.VMEM((4, 2, 128, 1408), BF),
            pltpu.VMEM((4, 2, 128, 1408), BF),
            pltpu.VMEM((4, 2, 176, 1024), BF),
            pltpu.VMEM((4, 2, 176, 1024), BF),
            pltpu.VMEM((128, 4096), BF),
            pltpu.VMEM((128, 1408), F32),
            pltpu.VMEM((176, 1024), F32),
            dma((NZ,)),
            dma((NZ,)),
            dma((4, 2, 2, 2)),
            dma((4, 2, 2, 2)),
            dma((2, 5, 4)),
            dma((2, 5, 4)),
            dma((2, 16)),
            dma((2, 16)),
            dma((NE,)),
            dma((NE,)),
            dma((NE,)),
            dma((NE,)),
            dma((NE,)),
            dma((NE,)),
            dma((4, 2, 2, 2)),
            dma((4, 2, 2, 2)),
            dma((8,)),
        ],
        compiler_params=pltpu.CompilerParams(
            collective_id=0, has_side_effects=True, vmem_limit_bytes=60 * 1024 * 1024
        ),
        name="moe_backward",
    )(tokens, proj, w1, w2, ids.T, gate.T, cot)
    return hand_out(*results)


def hand_kernel(*refs):
    sources, targets, held, sem = refs[:3], refs[3:6], refs[6:9], refs[9]
    take = [pltpu.make_async_copy(sources[i], held[i], sem.at[0, i]) for i in range(3)]
    give = [pltpu.make_async_copy(held[i], targets[i], sem.at[1, i]) for i in range(3)]
    for copy in take:
        copy.start()
    for i in range(3):
        take[i].wait()
        give[i].start()
    for copy in give:
        copy.wait()


def hand_out(*results):
    anywhere = pl.BlockSpec(memory_space=pl.ANY)
    return pl.pallas_call(
        hand_kernel,
        out_shape=tuple(jax.ShapeDtypeStruct(a.shape, a.dtype) for a in results),
        in_specs=[anywhere] * 3,
        out_specs=(anywhere,) * 3,
        scratch_shapes=[pltpu.VMEM(a.shape, a.dtype) for a in results]
        + [pltpu.SemaphoreType.DMA((2, 3))],
        compiler_params=pltpu.CompilerParams(vmem_limit_bytes=60 * 1024 * 1024),
        name="hand_out",
    )(*results)


def solution(mesh):
    return jax.shard_map(
        layer,
        mesh=mesh,
        in_specs=(
            P(("dp", "expert"), None),
            P(("dp", "expert"), None),
            P("expert", "dp", None),
            P("expert", "dp", None),
            P(("dp", "expert"), None),
            P(("dp", "expert"), None),
            P(("dp", "expert"), None),
        ),
        out_specs=(P(("dp", "expert"), None), P("expert", "dp", None), P("expert", "dp", None)),
        check_vma=False,
    )
```

```python
import jax
import jax.numpy as jnp
from jax import lax
from jax.experimental import pallas as pl
from jax.experimental.pallas import tpu as pltpu
from jax.sharding import PartitionSpec as P

GATE_DEN = 256
MESH = pl.DeviceIdType.MESH
BF = jnp.bfloat16
F32 = jnp.float32
NZ = 8
NX = 4
NE = 32
CAP = 24
SLOTS = NE * CAP
FAR_FIRST = (
    (2, 2),
    (2, 1),
    (2, 3),
    (1, 2),
    (3, 2),
    (2, 0),
    (0, 2),
    (1, 1),
    (3, 3),
    (1, 3),
    (3, 1),
    (1, 0),
    (3, 0),
    (0, 1),
    (0, 3),
)
ORDER = [(a, b, core) for core in (0, 1) for a, b in FAR_FIRST] + [(0, 0, 1)]


def contract_last(left, right):
    return lax.dot_general(
        left, right, (((1,), (1,)), ((), ())), preferred_element_type=jnp.float32
    )


def contract_first(left, right):
    return lax.dot_general(
        left, right, (((0,), (0,)), ((), ())), preferred_element_type=jnp.float32
    )


def enter(d, e):
    barrier = pltpu.get_barrier_semaphore()

    def greet_plane(i, carry):
        pl.semaphore_signal(
            barrier, inc=1, device_id=(d, lax.rem(e + i, NE)), device_id_type=MESH
        )
        return carry

    def greet_column(i, carry):
        pl.semaphore_signal(
            barrier, inc=1, device_id=(lax.rem(d + i, NZ), e), device_id_type=MESH
        )
        return carry

    lax.fori_loop(1, NE, greet_plane, 0)
    lax.fori_loop(1, NZ, greet_column, 0)
    pl.semaphore_wait(barrier, NE - 1 + NZ - 1)


def layer_kernel(
    tokens_in,
    proj_ref,
    w1_ref,
    w2_ref,
    ids_ref,
    gate_ref,
    cot_in,
    gt_out,
    g1_out,
    g2_out,
    col,
    w1_out,
    w2_out,
    lat_out,
    cot_out,
    tokens_ref,
    cot_ref,
    pick,
    acc,
    send_lat,
    send_cot,
    rows,
    rows_t,
    cots,
    hidden_t,
    active,
    grad_pre,
    back_send,
    back_recv,
    sum1_send,
    sum1_recv,
    sum2_send,
    sum2_recv,
    g1_stage,
    g2_stage,
    zp_send,
    zp_recv,
    wz_send,
    wz_recv,
    ax_send,
    ax_recv,
    mate_send,
    mate_recv,
    lat_send_sem,
    lat_recv_sem,
    cot_send_sem,
    cot_recv_sem,
    back_send_sem,
    back_recv_sem,
    sum_send,
    sum_recv,
    local_sem,
):
    d = lax.axis_index("dp")
    e = lax.axis_index("expert")
    x, y, c = e // 8, (e // 2) % NX, e % 2
    mate = (x * NX + y) * 2 + (1 - c)
    pending = []

    def remote(src, dst, ssem, rsem, dev):
        copy = pltpu.make_async_remote_copy(
            src_ref=src, dst_ref=dst, send_sem=ssem, recv_sem=rsem, device_id=dev, device_id_type=MESH
        )
        copy.start()
        pending.append(copy)
        return copy

    def arrived(dst, rsem):
        pltpu.make_async_remote_copy(
            src_ref=dst, dst_ref=dst, send_sem=rsem, recv_sem=rsem, device_id=(d, e), device_id_type=MESH
        ).wait_recv()

    fetch = [
        pltpu.make_async_copy(tokens_in, tokens_ref, local_sem.at[3]),
        pltpu.make_async_copy(cot_in, cot_ref, local_sem.at[4]),
    ]
    for copy in fetch:
        copy.start()
    own = [pltpu.make_async_copy(proj_ref, col.at[2, e], local_sem.at[0])]
    own[0].start()
    enter(d, e)

    own[0].wait()
    for i in (1, 7, 2, 4, 3, 5, 6):
        remote(
            col.at[2, e],
            col.at[(2 - i) % NZ, e],
            zp_send.at[i],
            zp_recv.at[i],
            (lax.rem(d + i, NZ), e),
        )

    weights = ((w1_ref, w1_out, 128), (w2_ref, w2_out, 176))
    def block_of(k, owner, first=0, count=None):
        span = weights[k][2]
        start = pl.multiple_of(owner * span + first, 16)
        return weights[k][1].at[pl.ds(start, span if count is None else count)]

    for k, (src, dst, _) in enumerate(weights):
        copy = pltpu.make_async_copy(src.at[0], block_of(k, d), local_sem.at[1 + k])
        copy.start()
        own.append(copy)
    right, left = lax.rem(d + 1, NZ), lax.rem(d + NZ - 1, NZ)

    cuts = (64, 96)

    def part_of(k, part):
        return (0, cuts[k]) if part == 0 else (cuts[k], weights[k][2] - cuts[k])

    def ring_send(s, k, part, way):
        owner = lax.rem(d - s + NZ, NZ) if way == 0 else lax.rem(d + s, NZ)
        to = (right, e) if way == 0 else (left, e)
        first, count = part_of(k, part)
        target = block_of(k, owner, first, count)
        source = weights[k][0].at[0, pl.ds(first, count)] if s == 0 else target
        remote(source, target, wz_send.at[s, k, part, way], wz_recv.at[s, k, part, way], to)

    def ring_first(k, part):
        for way in (0, 1):
            ring_send(0, k, part, way)

    def ring_step(s, k, part):
        for way in (0, 1):
            if s == 3 and way != part:
                continue
            owner = lax.rem(d - s - 1 + NZ, NZ) if way == 0 else lax.rem(d + s + 1, NZ)
            arrived(block_of(k, owner, *part_of(k, part)), wz_recv.at[s, k, part, way])
            if s < 2 or (s == 2 and way == part):
                ring_send(s + 1, k, part, way)

    slot = lax.broadcasted_iota(jnp.int32, (SLOTS, 128), 0)
    of_expert = (slot * 2731) >> 16
    rank_in = (slot - of_expert * CAP).astype(F32)
    named = jnp.zeros((SLOTS, 128), F32)
    gates = jnp.zeros((SLOTS, 128), F32)
    for k in range(4):
        hit = ids_ref[k : k + 1, :] == of_expert
        named = jnp.where(hit, 1.0, named)
        gates = jnp.where(hit, gate_ref[k : k + 1, :].astype(F32) * (1.0 / GATE_DEN), gates)
    before = lax.broadcasted_iota(jnp.int32, (128, 128), 0) < lax.broadcasted_iota(
        jnp.int32, (128, 128), 1
    )
    rank = jnp.dot(named.astype(BF), jnp.where(before, 1.0, 0.0).astype(BF), preferred_element_type=F32)
    chosen = jnp.logical_and(named > 0.0, rank == rank_in)
    one_hot = jnp.where(chosen, 1.0, 0.0)
    pick[0] = one_hot.astype(BF)
    pick[1] = jnp.where(chosen, gates, 0.0).astype(BF)
    for copy in fetch:
        copy.wait()
    ring_first(0, 0)

    def pack(which, rows_ref, out):
        for j in range(4):
            block = jnp.dot(
                pick[which, 192 * j : 192 * (j + 1), :], rows_ref[...], preferred_element_type=F32
            )
            for i in range(8):
                out[8 * j + i] = block[CAP * i : CAP * (i + 1), :].astype(BF)

    def away(n):
        dx, dy, dc = ORDER[n]
        core = c if dc == 0 else 1 - c
        to = (lax.rem(x + dx, NX) * NX + lax.rem(y + dy, NX)) * 2 + core
        source = (lax.rem(x - dx + NX, NX) * NX + lax.rem(y - dy + NX, NX)) * 2 + core
        return to, source

    def dispatch(buf, out, ssem, rsem, lo=0, hi=NE - 1):
        for n in range(lo, hi):
            to = away(n)[0]
            pltpu.make_async_remote_copy(
                src_ref=buf.at[to],
                dst_ref=out.at[e],
                send_sem=ssem.at[n],
                recv_sem=rsem.at[n],
                device_id=(d, to),
                device_id_type=MESH,
            ).start()
        if hi == NE - 1:
            pltpu.make_async_copy(buf.at[e], out.at[e], rsem.at[hi]).start()

    def landed(buf, out, ssem, rsem):
        for n in range(NE - 1):
            to, source = away(n)
            copy = pltpu.make_async_remote_copy(
                src_ref=buf.at[to],
                dst_ref=out.at[source],
                send_sem=ssem.at[n],
                recv_sem=rsem.at[n],
                device_id=(d, to),
                device_id_type=MESH,
            )
            copy.wait_send()
            copy.wait_recv()
        pltpu.make_async_copy(buf.at[e], out.at[e], rsem.at[NE - 1]).wait()

    pack(1, cot_ref, send_cot)
    ring_first(0, 1)
    dispatch(send_cot, cot_out, cot_send_sem, cot_recv_sem, 0, 15)

    def column(distances):
        for i in distances:
            arrived(col.at[(2 - i) % NZ, e], zp_recv.at[i])

    pos = ((x, y), (y, x))

    def device(h, p, q):
        p, q = lax.rem(p + 2 * NX, NX), lax.rem(q + 2 * NX, NX)
        return (p * NX + q) * 2 + c if h == 0 else (q * NX + p) * 2 + c

    def piece(h, who, sub=None):
        if sub is None:
            return col.at[pl.ds(4 * h, 4), who]
        return col.at[pl.ds(4 * h + 2 * sub, 2), who]

    def share(h, who, n):
        remote(piece(h, who), piece(h, who), mate_send.at[h, n], mate_recv.at[h, n], (d, mate))

    def spread(h, axis, who, n, sub=None, way=None):
        p, q = pos[h]
        for w in (0, 1) if way is None else (way,):
            step = 1 - 2 * w
            to = device(h, p + step, q) if axis == 0 else device(h, p, q + step)
            m = w if sub is None else 2 + w
            remote(
                piece(h, who, sub),
                piece(h, who, sub),
                ax_send.at[h, n, m],
                ax_recv.at[h, n, m],
                (d, to),
            )

    for h in (0, 1):
        column((3, 4, 5, 6) if h else (1, 2, 7))
        p, q = pos[h]
        spread(h, 0, device(h, p, q), 0)
        spread(h, 1, device(h, p, q), 1)
        share(h, device(h, p, q), 0)
    ring_first(1, 0)
    ring_first(1, 1)
    ring_step(0, 0, 0)
    for h in (0, 1):
        p, q = pos[h]
        for w in (0, 1):
            who = device(h, p - 1 + 2 * w, q)
            arrived(piece(h, who), ax_recv.at[h, 0, w])
            spread(h, 0, who, 0, sub=w, way=w)
            spread(h, 1, who, 2 + w)
            share(h, who, 1 + w)
    ring_step(0, 0, 1)
    for h in (0, 1):
        p, q = pos[h]
        who = device(h, p + 2, q)
        for w in (0, 1):
            arrived(piece(h, who, w), ax_recv.at[h, 0, 2 + w])
        spread(h, 1, who, 4)
        share(h, who, 3)
    ring_step(0, 1, 0)

    def second_stage(n):
        for h in (0, 1):
            p, q = pos[h]
            r = p + (0, -1, 1, 2)[n]
            for w in (0, 1):
                who = device(h, r, q - 1 + 2 * w)
                arrived(piece(h, who), ax_recv.at[h, 1 + n, w])
                spread(h, 1, who, 1 + n, sub=w, way=w)
                share(h, who, 4 + 3 * n + w)

    def second_stage_far(h, n):
        p, q = pos[h]
        r = p + (0, -1, 1, 2)[n]
        who = device(h, r, q + 2)
        for w in (0, 1):
            arrived(piece(h, who, w), ax_recv.at[h, 1 + n, 2 + w])
        share(h, who, 6 + 3 * n)

    second_stage(0)
    ring_step(0, 1, 1)
    second_stage(1)
    second_stage(2)
    ring_step(1, 0, 0)
    second_stage(3)
    dispatch(send_cot, cot_out, cot_send_sem, cot_recv_sem, 15)
    ring_step(1, 0, 1)

    def other(h, p, q):
        p, q = lax.rem(p + 2 * NX, NX), lax.rem(q + 2 * NX, NX)
        return ((p * NX + q) if h == 0 else (q * NX + p)) * 2 + (1 - c)

    order = [(0, 0), (-1, 0), (1, 0), (2, 0)]
    for n in range(4):
        r = (0, -1, 1, 2)[n]
        order += [(r, -1), (r, 1), (r, 2)]

    def other_core(h):
        p, q = pos[h]
        for n, (a, b) in enumerate(order):
            arrived(piece(h, other(h, p + a, q + b)), mate_recv.at[h, n])

    def half(n):
        return slice(512 * n, 512 * (n + 1))

    def plane(r):
        return pl.ds(pl.multiple_of(lax.rem(d + r + NZ - 2, NZ) * 512, 512), 512)

    def latent_sum(n, h):
        def step(r, carry):
            block = col[r, :, :, half(n)].reshape(512, 512)
            acc[n] += jnp.dot(tokens_ref[:, plane(r)], block, preferred_element_type=F32)
            return carry

        lax.fori_loop(4 * h, 4 * h + 4, step, 0)

    def latent_half(n):
        latent_sum(n, 1)
        latent = acc[n].astype(BF)
        for j in range(4):
            block = jnp.dot(
                pick[0, 192 * j : 192 * (j + 1), :], latent, preferred_element_type=F32
            )
            for i in range(8):
                send_lat[n, 8 * j + i] = block[CAP * i : CAP * (i + 1), :].astype(BF)
        dispatch(
            send_lat.at[n], lat_out.at[n], lat_send_sem.at[n], lat_recv_sem.at[n]
        )

    acc[...] = jnp.zeros_like(acc)
    for n in range(4):
        second_stage_far(0, n)
    other_core(0)
    for n in (0, 1):
        latent_sum(n, 0)
    for n in range(4):
        second_stage_far(1, n)
    ring_step(1, 1, 0)
    other_core(1)
    latent_half(0)
    ring_step(1, 1, 1)
    latent_half(1)
    ring_step(2, 0, 0)
    ring_step(2, 0, 1)

    def repack(buf, out, columns=slice(None)):
        def go(j, carry):
            pair = jnp.concatenate([buf[2 * j].astype(F32), buf[2 * j + 1].astype(F32)], axis=0)
            out[pl.ds(pl.multiple_of(j * 48, 16), 48), columns] = pair.astype(BF)
            return carry

        lax.fori_loop(0, NE // 2, go, 0)

    landed(send_cot, cot_out, cot_send_sem, cot_recv_sem)
    repack(cot_out, cots)
    ring_step(2, 1, 0)
    ring_step(2, 1, 1)
    ring_step(3, 0, 0)
    ring_step(3, 0, 1)
    own[1].wait()

    def tiles(tile):
        def go(j, carry):
            tile(pl.ds(pl.multiple_of(j * 256, 256), 256))
            return carry

        lax.fori_loop(0, 5, go, 0)
        tile(slice(1280, 1408))

    def latents_in(n):
        landed(send_lat.at[n], lat_out.at[n], lat_send_sem.at[n], lat_recv_sem.at[n])
        repack(lat_out.at[n], rows, half(n))

    def turn(n):
        def go(j, carry):
            part = pl.ds(pl.multiple_of(j * 128, 128), 128)
            rows_t[half(n), part] = rows[part, half(n)].T
            return carry

        lax.fori_loop(0, SLOTS // 128, go, 0)

    def preact_tile(part):
        active[:, part] = jnp.dot(
            rows[:, half(0)], w1_out[half(0), part], preferred_element_type=F32
        )

    def hidden_tile(part):
        preact = active[:, part] + jnp.dot(
            rows[:, half(1)], w1_out[half(1), part], preferred_element_type=F32
        )
        positive = jnp.maximum(preact, 0.0)
        active[:, part] = positive
        hidden_t[part, :] = (positive * positive).astype(BF).T

    def grad_tile(part):
        grad_hidden = contract_last(cots[...], w2_out[part, :])
        grad_pre[:, part] = (grad_hidden * 2.0 * active[:, part]).astype(BF)

    latents_in(0)
    tiles(preact_tile)
    turn(0)
    latents_in(1)
    tiles(hidden_tile)

    sums = (
        (sum1_send, sum1_recv, g1_stage, 128),
        (sum2_send, sum2_recv, g2_stage, 176),
    )

    def partial_of(k, owner):
        if k == 0:
            block = rows_t[pl.ds(pl.multiple_of(owner * 128, 128), 128), :]
            return jnp.dot(block, grad_pre[...], preferred_element_type=F32)
        block = hidden_t[pl.ds(pl.multiple_of(owner * 176, 16), 176), :]
        return jnp.dot(block, cots[...], preferred_element_type=F32)

    def sum_copy(s, k, part, way):
        out, inp = sums[k][:2]
        first, count = part_of(k, part)
        span = pl.ds(first, count)
        return pltpu.make_async_remote_copy(
            src_ref=out.at[s, way, span],
            dst_ref=inp.at[s, way, span],
            send_sem=sum_send.at[s, k, part, way],
            recv_sem=sum_recv.at[s, k, part, way],
            device_id=((right if way == 0 else left), e),
            device_id_type=MESH,
        )

    def sum_send_off(s, k, part, way):
        copy = sum_copy(s, k, part, way)
        copy.start()
        pending.append(copy)

    def sum_first(k):
        out = sums[k][0]
        block = partial_of(k, lax.rem(d + 4, NZ)).astype(BF)
        for way in (0, 1):
            first, count = part_of(k, way)
            out[0, way, first : first + count, :] = block[first : first + count, :]
            sum_send_off(0, k, way, way)

    def prepare(s, k):
        out, _, stage, _ = sums[k]
        if s == 4:
            stage[...] = partial_of(k, d)
            return
        for way in (0, 1):
            owner = lax.rem(d + 4 - s, NZ) if way == 0 else lax.rem(d + 4 + s, NZ)
            out[s, way] = partial_of(k, owner).astype(BF)

    def finish(s, k):
        out, inp, stage, _ = sums[k]
        for n in (0, 1):
            for way in (0, 1):
                part = 1 - way if n == 0 else way
                first, count = part_of(k, part)
                span = slice(first, first + count)
                sum_copy(s - 1, k, part, way).wait_recv()
                more = inp[s - 1, way, span, :].astype(F32)
                if s == 4:
                    stage[span, :] += more
                else:
                    out[s, way, span, :] = (out[s, way, span, :].astype(F32) + more).astype(BF)
                    sum_send_off(s, k, part, way)

    def sum_start(k):
        out, inp, stage, _ = sums[k]
        sum_first(k)
        for way in (0, 1):
            block = partial_of(k, lax.rem(d + 3, NZ) if way == 0 else lax.rem(d + 5, NZ))
            first, count = part_of(k, 1 - way)
            span = slice(first, first + count)
            out[1, way, span, :] = block[span, :].astype(BF)
            sum_send_off(1, k, 1 - way, way)
            first, count = part_of(k, way)
            span = slice(first, first + count)
            stage[span, :] = block[span, :]

    def sum_second(k):
        out, inp, stage, _ = sums[k]
        for way in (0, 1):
            first, count = part_of(k, way)
            span = slice(first, first + count)
            sum_copy(0, k, way, way).wait_recv()
            value = stage[span, :] + inp[0, way, span, :].astype(F32)
            out[1, way, span, :] = value.astype(BF)
            sum_send_off(1, k, way, way)

    sum_start(1)
    ring_step(3, 1, 0)
    ring_step(3, 1, 1)
    own[2].wait()
    tiles(grad_tile)
    turn(1)
    sum_start(0)
    sum_second(1)

    def route_tile(n, carry):
        part = pl.ds(pl.multiple_of(n * 256, 256), 256)
        block = contract_last(grad_pre[...], w1_out[part, :])
        for i in range(NE):
            back_send[i, :, part] = block[CAP * i : CAP * (i + 1), :].astype(BF)
        return carry

    lax.fori_loop(0, 4, route_tile, 0)
    dispatch(back_send, back_recv, back_send_sem, back_recv_sem)
    prepare(2, 1)
    sum_second(0)
    prepare(2, 0)
    finish(2, 1)
    prepare(3, 1)
    finish(2, 0)
    prepare(3, 0)
    prepare(4, 1)
    finish(3, 1)
    prepare(4, 0)
    finish(3, 0)
    early = len(pending) - 8
    for copy in pending[:early]:
        copy.wait_send()
    landed(back_send, back_recv, back_send_sem, back_recv_sem)
    repack(back_recv, rows)
    token_grad = contract_first(pick[0], rows[...]).astype(BF)

    def token_tile(j, carry):
        block = contract_last(token_grad, col[j].reshape(512, 1024))
        tokens_ref[:, plane(j)] = block.astype(BF)
        return carry

    lax.fori_loop(0, NZ, token_tile, 0)
    leave = [pltpu.make_async_copy(tokens_ref, gt_out, local_sem.at[5])]
    leave[0].start()
    finish(4, 1)
    leave.append(pltpu.make_async_copy(g2_stage, g2_out.at[0], local_sem.at[6]))
    leave[1].start()
    finish(4, 0)
    leave.append(pltpu.make_async_copy(g1_stage, g1_out.at[0], local_sem.at[7]))
    leave[2].start()
    for copy in pending[early:]:
        copy.wait_send()
    for copy in leave:
        copy.wait()


def layer(tokens, proj, w1, w2, ids, gate, cot):
    anywhere = pl.BlockSpec(memory_space=pl.ANY)
    vmem = pl.BlockSpec(memory_space=pltpu.VMEM)
    dma = pltpu.SemaphoreType.DMA
    slots = (NE, CAP, 1024)
    halves = (2, NE, CAP, 512)
    flat = (SLOTS, 1024)
    results = pl.pallas_call(
        layer_kernel,
        out_shape=(
            jax.ShapeDtypeStruct((128, 4096), BF),
            jax.ShapeDtypeStruct((1, 128, 1408), F32),
            jax.ShapeDtypeStruct((1, 176, 1024), F32),
        ),
        in_specs=[anywhere, anywhere, anywhere, anywhere, vmem, vmem, anywhere],
        out_specs=(anywhere,) * 3,
        scratch_shapes=[
            pltpu.VMEM((NZ, NE, 16, 1024), BF),
            pltpu.VMEM((1024, 1408), BF),
            pltpu.VMEM((1408, 1024), BF),
            pltpu.VMEM(halves, BF),
            pltpu.VMEM(slots, BF),
            pltpu.VMEM((128, 4096), BF),
            pltpu.VMEM((128, 1024), BF),
            pltpu.VMEM((2, SLOTS, 128), BF),
            pltpu.VMEM((2, 128, 512), F32),
            pltpu.VMEM(halves, BF),
            pltpu.VMEM(slots, BF),
            pltpu.VMEM(flat, BF),
            pltpu.VMEM((1024, SLOTS), BF),
            pltpu.VMEM(flat, BF),
            pltpu.VMEM((1408, SLOTS), BF),
            pltpu.VMEM((SLOTS, 1408), F32),
            pltpu.VMEM((SLOTS, 1408), BF),
            pltpu.VMEM(slots, BF),
            pltpu.VMEM(slots, BF),
            pltpu.VMEM((4, 2, 128, 1408), BF),
            pltpu.VMEM((4, 2, 128, 1408), BF),
            pltpu.VMEM((4, 2, 176, 1024), BF),
            pltpu.VMEM((4, 2, 176, 1024), BF),
            pltpu.VMEM((128, 1408), F32),
            pltpu.VMEM((176, 1024), F32),
            dma((NZ,)),
            dma((NZ,)),
            dma((4, 2, 2, 2)),
            dma((4, 2, 2, 2)),
            dma((2, 5, 4)),
            dma((2, 5, 4)),
            dma((2, 16)),
            dma((2, 16)),
            dma((2, NE)),
            dma((2, NE)),
            dma((NE,)),
            dma((NE,)),
            dma((NE,)),
            dma((NE,)),
            dma((4, 2, 2, 2)),
            dma((4, 2, 2, 2)),
            dma((8,)),
        ],
        compiler_params=pltpu.CompilerParams(
            collective_id=0, has_side_effects=True, vmem_limit_bytes=60 * 1024 * 1024
        ),
        name="moe_backward",
    )(tokens, proj, w1, w2, ids.T, gate.T, cot)
    return hand_out(*results)


def hand_kernel(*refs):
    sources, targets, held, sem = refs[:3], refs[3:6], refs[6:9], refs[9]
    take = [pltpu.make_async_copy(sources[i], held[i], sem.at[0, i]) for i in range(3)]
    give = [pltpu.make_async_copy(held[i], targets[i], sem.at[1, i]) for i in range(3)]
    for copy in take:
        copy.start()
    for i in range(3):
        take[i].wait()
        give[i].start()
    for copy in give:
        copy.wait()


def hand_out(*results):
    anywhere = pl.BlockSpec(memory_space=pl.ANY)
    return pl.pallas_call(
        hand_kernel,
        out_shape=tuple(jax.ShapeDtypeStruct(a.shape, a.dtype) for a in results),
        in_specs=[anywhere] * 3,
        out_specs=(anywhere,) * 3,
        scratch_shapes=[pltpu.VMEM(a.shape, a.dtype) for a in results]
        + [pltpu.SemaphoreType.DMA((2, 3))],
        compiler_params=pltpu.CompilerParams(vmem_limit_bytes=60 * 1024 * 1024),
        name="hand_out",
    )(*results)


def solution(mesh):
    return jax.shard_map(
        layer,
        mesh=mesh,
        in_specs=(
            P(("dp", "expert"), None),
            P(("dp", "expert"), None),
            P("expert", "dp", None),
            P("expert", "dp", None),
            P(("dp", "expert"), None),
            P(("dp", "expert"), None),
            P(("dp", "expert"), None),
        ),
        out_specs=(P(("dp", "expert"), None), P("expert", "dp", None), P("expert", "dp", None)),
        check_vma=False,
    )
```

```python
import jax
import jax.numpy as jnp
from jax import lax
from jax.experimental import pallas as pl
from jax.experimental.pallas import tpu as pltpu
from jax.sharding import PartitionSpec as P

GATE_DEN = 256
MESH = pl.DeviceIdType.MESH
BF = jnp.bfloat16
F32 = jnp.float32
NZ = 8
NX = 4
NE = 32
CAP = 24
SLOTS = NE * CAP
DEPTH = 4
FAR_FIRST = (
    (2, 2),
    (2, 1),
    (2, 3),
    (1, 2),
    (3, 2),
    (2, 0),
    (0, 2),
    (1, 1),
    (3, 3),
    (1, 3),
    (3, 1),
    (1, 0),
    (3, 0),
    (0, 1),
    (0, 3),
)
ORDER = [(a, b, core) for core in (0, 1) for a, b in FAR_FIRST] + [(0, 0, 1)]


def contract_last(left, right):
    return lax.dot_general(
        left, right, (((1,), (1,)), ((), ())), preferred_element_type=jnp.float32
    )


def contract_first(left, right):
    return lax.dot_general(
        left, right, (((0,), (0,)), ((), ())), preferred_element_type=jnp.float32
    )


def enter(d, e):
    barrier = pltpu.get_barrier_semaphore()

    def greet_plane(i, carry):
        pl.semaphore_signal(
            barrier, inc=1, device_id=(d, lax.rem(e + i, NE)), device_id_type=MESH
        )
        return carry

    def greet_column(i, carry):
        pl.semaphore_signal(
            barrier, inc=1, device_id=(lax.rem(d + i, NZ), e), device_id_type=MESH
        )
        return carry

    lax.fori_loop(1, NE, greet_plane, 0)
    lax.fori_loop(1, NZ, greet_column, 0)
    pl.semaphore_wait(barrier, NE - 1 + NZ - 1)


def layer_kernel(
    tokens_in,
    proj_ref,
    w1_ref,
    w2_ref,
    ids_ref,
    gate_ref,
    cot_in,
    gt_out,
    g1_out,
    g2_out,
    col,
    w1_out,
    w2_out,
    lat_out,
    cot_out,
    tokens_ref,
    cot_ref,
    pick,
    acc,
    send_lat,
    send_cot,
    rows,
    rows_t,
    cots,
    hidden_t,
    active,
    grad_pre,
    back_send,
    back_recv,
    sum1_send,
    sum1_recv,
    sum2_send,
    sum2_recv,
    g1_stage,
    g2_stage,
    zp_send,
    zp_recv,
    wz_send,
    wz_recv,
    ax_send,
    ax_recv,
    mate_send,
    mate_recv,
    lat_send_sem,
    lat_recv_sem,
    cot_send_sem,
    cot_recv_sem,
    back_send_sem,
    back_recv_sem,
    sum_send,
    sum_recv,
    local_sem,
):
    d = lax.axis_index("dp")
    e = lax.axis_index("expert")
    x, y, c = e // 8, (e // 2) % NX, e % 2
    mate = (x * NX + y) * 2 + (1 - c)
    pending = []

    def remote(src, dst, ssem, rsem, dev):
        copy = pltpu.make_async_remote_copy(
            src_ref=src, dst_ref=dst, send_sem=ssem, recv_sem=rsem, device_id=dev, device_id_type=MESH
        )
        copy.start()
        pending.append(copy)
        return copy

    def arrived(dst, rsem):
        pltpu.make_async_remote_copy(
            src_ref=dst, dst_ref=dst, send_sem=rsem, recv_sem=rsem, device_id=(d, e), device_id_type=MESH
        ).wait_recv()

    fetch = [
        pltpu.make_async_copy(tokens_in, tokens_ref, local_sem.at[3]),
        pltpu.make_async_copy(cot_in, cot_ref, local_sem.at[4]),
    ]
    for copy in fetch:
        copy.start()
    own = [pltpu.make_async_copy(proj_ref, col.at[2, e], local_sem.at[0])]
    own[0].start()
    enter(d, e)

    own[0].wait()
    for i in (1, 7, 2, 4, 3, 5, 6):
        remote(
            col.at[2, e],
            col.at[(2 - i) % NZ, e],
            zp_send.at[i],
            zp_recv.at[i],
            (lax.rem(d + i, NZ), e),
        )

    weights = ((w1_ref, w1_out, 128), (w2_ref, w2_out, 176))
    def block_of(k, owner, first=0, count=None):
        span = weights[k][2]
        start = pl.multiple_of(owner * span + first, 16)
        held = weights[k][1]
        part = pl.ds(start, span if count is None else count)
        return held.at[part, pl.ds(0, 1408)] if k == 0 else held.at[part]

    for k, (src, dst, _) in enumerate(weights):
        copy = pltpu.make_async_copy(src.at[0], block_of(k, d), local_sem.at[1 + k])
        copy.start()
        own.append(copy)
    right, left = lax.rem(d + 1, NZ), lax.rem(d + NZ - 1, NZ)

    cuts = (64, 96)

    def part_of(k, part):
        return (0, cuts[k]) if part == 0 else (cuts[k], weights[k][2] - cuts[k])

    def ring_send(s, k, part, way):
        owner = lax.rem(d - s + NZ, NZ) if way == 0 else lax.rem(d + s, NZ)
        to = (right, e) if way == 0 else (left, e)
        first, count = part_of(k, part)
        target = block_of(k, owner, first, count)
        source = weights[k][0].at[0, pl.ds(first, count)] if s == 0 else target
        remote(source, target, wz_send.at[s, k, part, way], wz_recv.at[s, k, part, way], to)

    def ring_first(k, part):
        for way in (0, 1):
            ring_send(0, k, part, way)

    def ring_step(s, k, part):
        for way in (0, 1):
            if s == 3 and way != part:
                continue
            owner = lax.rem(d - s - 1 + NZ, NZ) if way == 0 else lax.rem(d + s + 1, NZ)
            arrived(block_of(k, owner, *part_of(k, part)), wz_recv.at[s, k, part, way])
            if s < 2 or (s == 2 and way == part):
                ring_send(s + 1, k, part, way)

    slot = lax.broadcasted_iota(jnp.int32, (SLOTS, 128), 0)
    of_expert = (slot * 2731) >> 16
    rank_in = (slot - of_expert * CAP).astype(F32)
    named = jnp.zeros((SLOTS, 128), F32)
    gates = jnp.zeros((SLOTS, 128), F32)
    for k in range(4):
        hit = ids_ref[k : k + 1, :] == of_expert
        named = jnp.where(hit, 1.0, named)
        gates = jnp.where(hit, gate_ref[k : k + 1, :].astype(F32) * (1.0 / GATE_DEN), gates)
    before = lax.broadcasted_iota(jnp.int32, (128, 128), 0) < lax.broadcasted_iota(
        jnp.int32, (128, 128), 1
    )
    rank = jnp.dot(named.astype(BF), jnp.where(before, 1.0, 0.0).astype(BF), preferred_element_type=F32)
    chosen = jnp.logical_and(named > 0.0, rank == rank_in)
    one_hot = jnp.where(chosen, 1.0, 0.0)
    pick[0] = one_hot.astype(BF)
    pick[1] = jnp.where(chosen, gates, 0.0).astype(BF)
    for copy in fetch:
        copy.wait()
    ring_first(0, 0)

    def pack(which, rows_ref, out):
        for j in range(4):
            block = jnp.dot(
                pick[which, 192 * j : 192 * (j + 1), :], rows_ref[...], preferred_element_type=F32
            )
            for i in range(8):
                out[8 * j + i] = block[CAP * i : CAP * (i + 1), :].astype(BF)

    def away(n):
        dx, dy, dc = ORDER[n]
        core = c if dc == 0 else 1 - c
        to = (lax.rem(x + dx, NX) * NX + lax.rem(y + dy, NX)) * 2 + core
        source = (lax.rem(x - dx + NX, NX) * NX + lax.rem(y - dy + NX, NX)) * 2 + core
        return to, source

    def dispatch(buf, out, ssem, rsem, lo=0, hi=NE - 1):
        for n in range(lo, hi):
            to = away(n)[0]
            pltpu.make_async_remote_copy(
                src_ref=buf.at[to],
                dst_ref=out.at[e],
                send_sem=ssem.at[n],
                recv_sem=rsem.at[n],
                device_id=(d, to),
                device_id_type=MESH,
            ).start()
        if hi == NE - 1:
            pltpu.make_async_copy(buf.at[e], out.at[e], rsem.at[hi]).start()

    def landed(buf, out, ssem, rsem):
        for n in range(NE - 1):
            to, source = away(n)
            copy = pltpu.make_async_remote_copy(
                src_ref=buf.at[to],
                dst_ref=out.at[source],
                send_sem=ssem.at[n],
                recv_sem=rsem.at[n],
                device_id=(d, to),
                device_id_type=MESH,
            )
            copy.wait_send()
            copy.wait_recv()
        pltpu.make_async_copy(buf.at[e], out.at[e], rsem.at[NE - 1]).wait()

    pack(1, cot_ref, send_cot)
    ring_first(0, 1)
    dispatch(send_cot, cot_out, cot_send_sem, cot_recv_sem, 0, 15)

    def column(distances):
        for i in distances:
            arrived(col.at[(2 - i) % NZ, e], zp_recv.at[i])

    pos = ((x, y), (y, x))

    def device(h, p, q):
        p, q = lax.rem(p + 2 * NX, NX), lax.rem(q + 2 * NX, NX)
        return (p * NX + q) * 2 + c if h == 0 else (q * NX + p) * 2 + c

    def piece(h, who, sub=None):
        if sub is None:
            return col.at[pl.ds(4 * h, 4), who]
        return col.at[pl.ds(4 * h + 2 * sub, 2), who]

    def share(h, who, n):
        remote(piece(h, who), piece(h, who), mate_send.at[h, n], mate_recv.at[h, n], (d, mate))

    def spread(h, axis, who, n, sub=None, way=None):
        p, q = pos[h]
        for w in (0, 1) if way is None else (way,):
            step = 1 - 2 * w
            to = device(h, p + step, q) if axis == 0 else device(h, p, q + step)
            m = w if sub is None else 2 + w
            remote(
                piece(h, who, sub),
                piece(h, who, sub),
                ax_send.at[h, n, m],
                ax_recv.at[h, n, m],
                (d, to),
            )

    for h in (0, 1):
        column((3, 4, 5, 6) if h else (1, 2, 7))
        p, q = pos[h]
        spread(h, 0, device(h, p, q), 0)
        spread(h, 1, device(h, p, q), 1)
        share(h, device(h, p, q), 0)
    ring_first(1, 0)
    ring_first(1, 1)
    ring_step(0, 0, 0)
    for h in (0, 1):
        p, q = pos[h]
        for w in (0, 1):
            who = device(h, p - 1 + 2 * w, q)
            arrived(piece(h, who), ax_recv.at[h, 0, w])
            spread(h, 0, who, 0, sub=w, way=w)
            spread(h, 1, who, 2 + w)
            share(h, who, 1 + w)
    ring_step(0, 0, 1)
    for h in (0, 1):
        p, q = pos[h]
        who = device(h, p + 2, q)
        for w in (0, 1):
            arrived(piece(h, who, w), ax_recv.at[h, 0, 2 + w])
        spread(h, 1, who, 4)
        share(h, who, 3)
    ring_step(0, 1, 0)

    def second_stage(n):
        for h in (0, 1):
            p, q = pos[h]
            r = p + (0, -1, 1, 2)[n]
            for w in (0, 1):
                who = device(h, r, q - 1 + 2 * w)
                arrived(piece(h, who), ax_recv.at[h, 1 + n, w])
                spread(h, 1, who, 1 + n, sub=w, way=w)
                share(h, who, 4 + 3 * n + w)

    def second_stage_far(h, n):
        p, q = pos[h]
        r = p + (0, -1, 1, 2)[n]
        who = device(h, r, q + 2)
        for w in (0, 1):
            arrived(piece(h, who, w), ax_recv.at[h, 1 + n, 2 + w])
        share(h, who, 6 + 3 * n)

    second_stage(0)
    ring_step(0, 1, 1)
    second_stage(1)
    second_stage(2)
    ring_step(1, 0, 0)
    second_stage(3)
    dispatch(send_cot, cot_out, cot_send_sem, cot_recv_sem, 15)
    ring_step(1, 0, 1)

    def other(h, p, q):
        p, q = lax.rem(p + 2 * NX, NX), lax.rem(q + 2 * NX, NX)
        return ((p * NX + q) if h == 0 else (q * NX + p)) * 2 + (1 - c)

    order = [(0, 0), (-1, 0), (1, 0), (2, 0)]
    for n in range(4):
        r = (0, -1, 1, 2)[n]
        order += [(r, -1), (r, 1), (r, 2)]

    def other_core(h):
        p, q = pos[h]
        for n, (a, b) in enumerate(order):
            arrived(piece(h, other(h, p + a, q + b)), mate_recv.at[h, n])

    def half(n):
        return slice(512 * n, 512 * (n + 1))

    def plane(r):
        return pl.ds(pl.multiple_of(lax.rem(d + r + NZ - 2, NZ) * 512, 512), 512)

    def latent_sum(n, h):
        def step(r, carry):
            block = col[r, :, :, half(n)].reshape(512, 512)
            acc[n] += jnp.dot(tokens_ref[:, plane(r)], block, preferred_element_type=F32)
            return carry

        lax.fori_loop(4 * h, 4 * h + 4, step, 0)

    def latent_half(n):
        latent_sum(n, 1)
        latent = acc[n].astype(BF)
        for j in range(4):
            block = jnp.dot(
                pick[0, 192 * j : 192 * (j + 1), :], latent, preferred_element_type=F32
            )
            for i in range(8):
                send_lat[n, 8 * j + i] = block[CAP * i : CAP * (i + 1), :].astype(BF)
        dispatch(
            send_lat.at[n], lat_out.at[n], lat_send_sem.at[n], lat_recv_sem.at[n]
        )

    acc[...] = jnp.zeros_like(acc)
    w1_out[:, 1408:] = jnp.zeros((1024, 128), BF)
    active[:, 1408:] = jnp.zeros((SLOTS, 128), F32)
    for n in range(4):
        second_stage_far(0, n)
    other_core(0)
    for n in (0, 1):
        latent_sum(n, 0)
    for n in range(4):
        second_stage_far(1, n)
    ring_step(1, 1, 0)
    other_core(1)
    latent_half(0)
    ring_step(1, 1, 1)
    latent_half(1)
    ring_step(2, 0, 0)
    ring_step(2, 0, 1)

    def repack(buf, out, columns=slice(None)):
        def go(j, carry):
            pair = jnp.concatenate([buf[2 * j].astype(F32), buf[2 * j + 1].astype(F32)], axis=0)
            out[pl.ds(pl.multiple_of(j * 48, 16), 48), columns] = pair.astype(BF)
            return carry

        lax.fori_loop(0, NE // 2, go, 0)

    landed(send_cot, cot_out, cot_send_sem, cot_recv_sem)
    repack(cot_out, cots)
    ring_step(2, 1, 0)
    ring_step(2, 1, 1)
    ring_step(3, 0, 0)
    ring_step(3, 0, 1)
    own[1].wait()

    def tiles(tile):
        def go(j, carry):
            tile(pl.ds(pl.multiple_of(j * 256, 256), 256))
            return carry

        lax.fori_loop(0, 5, go, 0)
        tile(slice(1280, 1408))

    def latents_in(n):
        landed(send_lat.at[n], lat_out.at[n], lat_send_sem.at[n], lat_recv_sem.at[n])
        repack(lat_out.at[n], rows, half(n))

    def turn(n):
        def go(j, carry):
            part = pl.ds(pl.multiple_of(j * 128, 128), 128)
            rows_t[half(n), part] = rows[part, half(n)].T
            return carry

        lax.fori_loop(0, SLOTS // 128, go, 0)

    def preact_tile(part):
        active[:, part] = jnp.dot(
            rows[:, half(0)], w1_out[half(0), part], preferred_element_type=F32
        )

    def hidden_tile(part):
        preact = active[:, part] + jnp.dot(
            rows[:, half(1)], w1_out[half(1), part], preferred_element_type=F32
        )
        positive = jnp.maximum(preact, 0.0)
        active[:, part] = positive
        hidden_t[part, :] = (positive * positive).astype(BF).T

    def grad_tile(part):
        grad_hidden = contract_last(cots[...], w2_out[part, :])
        grad_pre[:, part] = (grad_hidden * 2.0 * active[:, part]).astype(BF)

    latents_in(0)
    tiles(preact_tile)
    turn(0)
    latents_in(1)
    foremost = (176 * lax.rem(d + 4, NZ)) // 256

    def hidden_turn(j, carry):
        start = lax.rem(foremost + j, 6) * 256
        hidden_tile(pl.ds(pl.multiple_of(start, 256), 256))
        return carry

    lax.fori_loop(0, 2, hidden_turn, 0)

    sums = (
        (sum1_send, sum1_recv, g1_stage, 128),
        (sum2_send, sum2_recv, g2_stage, 176),
    )

    def partial_of(k, owner):
        if k == 0:
            block = rows_t[pl.ds(pl.multiple_of(owner * 128, 128), 128), :]
            return jnp.dot(block, grad_pre[...], preferred_element_type=F32)
        block = hidden_t[pl.ds(pl.multiple_of(owner * 176, 16), 176), :]
        return jnp.dot(block, cots[...], preferred_element_type=F32)

    def sum_copy(s, k, part, way):
        out, inp = sums[k][:2]
        first, count = part_of(k, part)
        span = pl.ds(first, count)
        return pltpu.make_async_remote_copy(
            src_ref=out.at[s, way, span],
            dst_ref=inp.at[s, way, span],
            send_sem=sum_send.at[s, k, part, way],
            recv_sem=sum_recv.at[s, k, part, way],
            device_id=((right if way == 0 else left), e),
            device_id_type=MESH,
        )

    flying = ([], [])

    def sum_send_off(s, k, part, way):
        if len(flying[way]) == DEPTH:
            flying[way].pop(0).wait_send()
        copy = sum_copy(s, k, part, way)
        copy.start()
        flying[way].append(copy)

    def prepare(s, k):
        out, _, stage, _ = sums[k]
        if s == 4:
            stage[...] = partial_of(k, d)
            return
        if s == 0:
            block = partial_of(k, lax.rem(d + 4, NZ)).astype(BF)
            for way in (0, 1):
                first, count = part_of(k, way)
                out[0, way, first : first + count, :] = block[first : first + count, :]
            return
        for way in (0, 1):
            owner = lax.rem(d + 4 - s, NZ) if way == 0 else lax.rem(d + 4 + s, NZ)
            out[s, way] = partial_of(k, owner).astype(BF)

    def push(s, k, late):
        out, inp, stage, _ = sums[k]
        for way in (0, 1):
            part = way if late else 1 - way
            first, count = part_of(k, part)
            span = slice(first, first + count)
            if s > 1 or (s == 1 and late):
                sum_copy(s - 1, k, part, way).wait_recv()
                more = inp[s - 1, way, span, :].astype(F32)
                if s == 4:
                    stage[span, :] += more
                else:
                    out[s, way, span, :] = (out[s, way, span, :].astype(F32) + more).astype(BF)
            if s < 4:
                sum_send_off(s, k, part, way)

    prepare(0, 1)
    push(0, 1, True)
    lax.fori_loop(2, 6, hidden_turn, 0)
    prepare(1, 1)
    push(1, 1, False)
    ring_step(3, 1, 0)
    ring_step(3, 1, 1)
    own[2].wait()
    tiles(grad_tile)
    turn(1)
    prepare(0, 0)
    push(0, 0, True)
    prepare(1, 0)
    push(1, 0, False)
    prepare(2, 1)
    push(1, 1, True)
    push(2, 1, False)

    def route_tile(n, carry):
        part = pl.ds(pl.multiple_of(n * 256, 256), 256)
        block = contract_last(grad_pre[...], w1_out[part, :1408])
        for i in range(NE):
            back_send[i, :, part] = block[CAP * i : CAP * (i + 1), :].astype(BF)
        return carry

    lax.fori_loop(0, 4, route_tile, 0)
    dispatch(back_send, back_recv, back_send_sem, back_recv_sem)
    prepare(2, 0)
    push(1, 0, True)
    push(2, 0, False)
    prepare(3, 1)
    push(2, 1, True)
    push(3, 1, False)
    prepare(3, 0)
    push(2, 0, True)
    push(3, 0, False)
    prepare(4, 1)
    prepare(4, 0)
    push(3, 1, True)
    push(3, 0, True)
    for copy in pending:
        copy.wait_send()
    landed(back_send, back_recv, back_send_sem, back_recv_sem)
    repack(back_recv, rows)
    token_grad = contract_first(pick[0], rows[...]).astype(BF)

    def token_tile(j, carry):
        block = contract_last(token_grad, col[j].reshape(512, 1024))
        tokens_ref[:, plane(j)] = block.astype(BF)
        return carry

    lax.fori_loop(0, NZ, token_tile, 0)
    leave = [pltpu.make_async_copy(tokens_ref, gt_out, local_sem.at[5])]
    leave[0].start()
    push(4, 1, False)
    push(4, 1, True)
    leave.append(pltpu.make_async_copy(g2_stage, g2_out.at[0], local_sem.at[6]))
    leave[1].start()
    push(4, 0, False)
    push(4, 0, True)
    leave.append(pltpu.make_async_copy(g1_stage, g1_out.at[0], local_sem.at[7]))
    leave[2].start()
    for copy in flying[0] + flying[1]:
        copy.wait_send()
    for copy in leave:
        copy.wait()


def layer(tokens, proj, w1, w2, ids, gate, cot):
    anywhere = pl.BlockSpec(memory_space=pl.ANY)
    vmem = pl.BlockSpec(memory_space=pltpu.VMEM)
    dma = pltpu.SemaphoreType.DMA
    slots = (NE, CAP, 1024)
    halves = (2, NE, CAP, 512)
    flat = (SLOTS, 1024)
    results = pl.pallas_call(
        layer_kernel,
        out_shape=(
            jax.ShapeDtypeStruct((128, 4096), BF),
            jax.ShapeDtypeStruct((1, 128, 1408), F32),
            jax.ShapeDtypeStruct((1, 176, 1024), F32),
        ),
        in_specs=[anywhere, anywhere, anywhere, anywhere, vmem, vmem, anywhere],
        out_specs=(anywhere,) * 3,
        scratch_shapes=[
            pltpu.VMEM((NZ, NE, 16, 1024), BF),
            pltpu.VMEM((1024, 1536), BF),
            pltpu.VMEM((1408, 1024), BF),
            pltpu.VMEM(halves, BF),
            pltpu.VMEM(slots, BF),
            pltpu.VMEM((128, 4096), BF),
            pltpu.VMEM((128, 1024), BF),
            pltpu.VMEM((2, SLOTS, 128), BF),
            pltpu.VMEM((2, 128, 512), F32),
            pltpu.VMEM(halves, BF),
            pltpu.VMEM(slots, BF),
            pltpu.VMEM(flat, BF),
            pltpu.VMEM((1024, SLOTS), BF),
            pltpu.VMEM(flat, BF),
            pltpu.VMEM((1536, SLOTS), BF),
            pltpu.VMEM((SLOTS, 1536), F32),
            pltpu.VMEM((SLOTS, 1408), BF),
            pltpu.VMEM(slots, BF),
            pltpu.VMEM(slots, BF),
            pltpu.VMEM((4, 2, 128, 1408), BF),
            pltpu.VMEM((4, 2, 128, 1408), BF),
            pltpu.VMEM((4, 2, 176, 1024), BF),
            pltpu.VMEM((4, 2, 176, 1024), BF),
            pltpu.VMEM((128, 1408), F32),
            pltpu.VMEM((176, 1024), F32),
            dma((NZ,)),
            dma((NZ,)),
            dma((4, 2, 2, 2)),
            dma((4, 2, 2, 2)),
            dma((2, 5, 4)),
            dma((2, 5, 4)),
            dma((2, 16)),
            dma((2, 16)),
            dma((2, NE)),
            dma((2, NE)),
            dma((NE,)),
            dma((NE,)),
            dma((NE,)),
            dma((NE,)),
            dma((4, 2, 2, 2)),
            dma((4, 2, 2, 2)),
            dma((8,)),
        ],
        compiler_params=pltpu.CompilerParams(
            collective_id=0, has_side_effects=True, vmem_limit_bytes=60 * 1024 * 1024
        ),
        name="moe_backward",
    )(tokens, proj, w1, w2, ids.T, gate.T, cot)
    return hand_out(*results)


def hand_kernel(*refs):
    sources, targets, held, sem = refs[:3], refs[3:6], refs[6:9], refs[9]

    def piece(ref, half):
        rows = ref.shape[-2] // 2
        part = pl.ds(half * rows, rows)
        return ref.at[part] if len(ref.shape) == 2 else ref.at[0, part]

    each = [(i, half) for i in range(3) for half in (0, 1)]
    take = [
        pltpu.make_async_copy(piece(sources[i], h), piece(held[i], h), sem.at[0, i, h])
        for i, h in each
    ]
    give = [
        pltpu.make_async_copy(piece(held[i], h), piece(targets[i], h), sem.at[1, i, h])
        for i, h in each
    ]
    for copy in take:
        copy.start()
    for came, goes in zip(take, give):
        came.wait()
        goes.start()
    for copy in give:
        copy.wait()


def hand_out(*results):
    anywhere = pl.BlockSpec(memory_space=pl.ANY)
    return pl.pallas_call(
        hand_kernel,
        out_shape=tuple(jax.ShapeDtypeStruct(a.shape, a.dtype) for a in results),
        in_specs=[anywhere] * 3,
        out_specs=(anywhere,) * 3,
        scratch_shapes=[pltpu.VMEM(a.shape, a.dtype) for a in results]
        + [pltpu.SemaphoreType.DMA((2, 3, 2))],
        compiler_params=pltpu.CompilerParams(vmem_limit_bytes=60 * 1024 * 1024),
        name="hand_out",
    )(*results)


def solution(mesh):
    return jax.shard_map(
        layer,
        mesh=mesh,
        in_specs=(
            P(("dp", "expert"), None),
            P(("dp", "expert"), None),
            P("expert", "dp", None),
            P("expert", "dp", None),
            P(("dp", "expert"), None),
            P(("dp", "expert"), None),
            P(("dp", "expert"), None),
        ),
        out_specs=(P(("dp", "expert"), None), P("expert", "dp", None), P("expert", "dp", None)),
        check_vma=False,
    )
```

```python
import jax
import jax.numpy as jnp
from jax import lax
from jax.experimental import pallas as pl
from jax.experimental.pallas import tpu as pltpu
from jax.sharding import PartitionSpec as P

GATE_DEN = 256
MESH = pl.DeviceIdType.MESH
BF = jnp.bfloat16
F32 = jnp.float32
NZ = 8
NX = 4
NE = 32
CAP = 24
SLOTS = NE * CAP
DEPTH = 4
FAR_FIRST = (
    (2, 2),
    (2, 1),
    (2, 3),
    (1, 2),
    (3, 2),
    (2, 0),
    (0, 2),
    (1, 1),
    (3, 3),
    (1, 3),
    (3, 1),
    (1, 0),
    (3, 0),
    (0, 1),
    (0, 3),
)
ORDER = [(a, b, core) for core in (0, 1) for a, b in FAR_FIRST] + [(0, 0, 1)]


def contract_last(left, right):
    return lax.dot_general(
        left, right, (((1,), (1,)), ((), ())), preferred_element_type=jnp.float32
    )


def contract_first(left, right):
    return lax.dot_general(
        left, right, (((0,), (0,)), ((), ())), preferred_element_type=jnp.float32
    )


def enter(d, e):
    barrier = pltpu.get_barrier_semaphore()

    def greet_plane(i, carry):
        pl.semaphore_signal(
            barrier, inc=1, device_id=(d, lax.rem(e + i, NE)), device_id_type=MESH
        )
        return carry

    def greet_column(i, carry):
        pl.semaphore_signal(
            barrier, inc=1, device_id=(lax.rem(d + i, NZ), e), device_id_type=MESH
        )
        return carry

    lax.fori_loop(1, NE, greet_plane, 0)
    lax.fori_loop(1, NZ, greet_column, 0)
    pl.semaphore_wait(barrier, NE - 1 + NZ - 1)


def layer_kernel(
    tokens_in,
    proj_ref,
    w1_ref,
    w2_ref,
    ids_ref,
    gate_ref,
    cot_in,
    gt_out,
    g1_out,
    g2_out,
    col,
    w1_out,
    w2_out,
    lat_out,
    cot_out,
    tokens_ref,
    cot_ref,
    pick,
    acc,
    send_lat,
    send_cot,
    rows,
    rows_t,
    cots,
    hidden_t,
    active,
    grad_pre,
    back_send,
    back_recv,
    sum1_send,
    sum1_recv,
    sum2_send,
    sum2_recv,
    g1_stage,
    g2_stage,
    zp_send,
    zp_recv,
    wz_send,
    wz_recv,
    ax_send,
    ax_recv,
    mate_send,
    mate_recv,
    lat_send_sem,
    lat_recv_sem,
    cot_send_sem,
    cot_recv_sem,
    back_send_sem,
    back_recv_sem,
    sum_send,
    sum_recv,
    local_sem,
):
    d = lax.axis_index("dp")
    e = lax.axis_index("expert")
    x, y, c = e // 8, (e // 2) % NX, e % 2
    mate = (x * NX + y) * 2 + (1 - c)
    pending = []

    def remote(src, dst, ssem, rsem, dev):
        copy = pltpu.make_async_remote_copy(
            src_ref=src, dst_ref=dst, send_sem=ssem, recv_sem=rsem, device_id=dev, device_id_type=MESH
        )
        copy.start()
        pending.append(copy)
        return copy

    def arrived(dst, rsem):
        pltpu.make_async_remote_copy(
            src_ref=dst, dst_ref=dst, send_sem=rsem, recv_sem=rsem, device_id=(d, e), device_id_type=MESH
        ).wait_recv()

    fetch = [
        pltpu.make_async_copy(tokens_in, tokens_ref, local_sem.at[3]),
        pltpu.make_async_copy(cot_in, cot_ref, local_sem.at[4]),
    ]
    for copy in fetch:
        copy.start()
    own = [pltpu.make_async_copy(proj_ref, col.at[2, e], local_sem.at[0])]
    own[0].start()
    enter(d, e)

    own[0].wait()
    for i in (1, 7, 2, 4, 3, 5, 6):
        remote(
            col.at[2, e],
            col.at[(2 - i) % NZ, e],
            zp_send.at[i],
            zp_recv.at[i],
            (lax.rem(d + i, NZ), e),
        )

    weights = ((w1_ref, w1_out, 128), (w2_ref, w2_out, 176))
    def block_of(k, owner, first=0, count=None):
        span = weights[k][2]
        start = pl.multiple_of(owner * span + first, 16)
        held = weights[k][1]
        part = pl.ds(start, span if count is None else count)
        return held.at[part, pl.ds(0, 1408)] if k == 0 else held.at[part]

    for k, (src, dst, _) in enumerate(weights):
        copy = pltpu.make_async_copy(src.at[0], block_of(k, d), local_sem.at[1 + k])
        copy.start()
        own.append(copy)
    right, left = lax.rem(d + 1, NZ), lax.rem(d + NZ - 1, NZ)

    cuts = (64, 96)

    def part_of(k, part):
        return (0, cuts[k]) if part == 0 else (cuts[k], weights[k][2] - cuts[k])

    def ring_send(s, k, part, way):
        owner = lax.rem(d - s + NZ, NZ) if way == 0 else lax.rem(d + s, NZ)
        to = (right, e) if way == 0 else (left, e)
        first, count = part_of(k, part)
        target = block_of(k, owner, first, count)
        source = weights[k][0].at[0, pl.ds(first, count)] if s == 0 else target
        remote(source, target, wz_send.at[s, k, part, way], wz_recv.at[s, k, part, way], to)

    def ring_first(k, part):
        for way in (0, 1):
            ring_send(0, k, part, way)

    def ring_step(s, k, part):
        for way in (0, 1):
            if s == 3 and way != part:
                continue
            owner = lax.rem(d - s - 1 + NZ, NZ) if way == 0 else lax.rem(d + s + 1, NZ)
            arrived(block_of(k, owner, *part_of(k, part)), wz_recv.at[s, k, part, way])
            if s < 2 or (s == 2 and way == part):
                ring_send(s + 1, k, part, way)

    slot = lax.broadcasted_iota(jnp.int32, (SLOTS, 128), 0)
    of_expert = (slot * 2731) >> 16
    rank_in = (slot - of_expert * CAP).astype(F32)
    named = jnp.zeros((SLOTS, 128), F32)
    gates = jnp.zeros((SLOTS, 128), F32)
    for k in range(4):
        hit = ids_ref[k : k + 1, :] == of_expert
        named = jnp.where(hit, 1.0, named)
        gates = jnp.where(hit, gate_ref[k : k + 1, :].astype(F32) * (1.0 / GATE_DEN), gates)
    before = lax.broadcasted_iota(jnp.int32, (128, 128), 0) < lax.broadcasted_iota(
        jnp.int32, (128, 128), 1
    )
    rank = jnp.dot(named.astype(BF), jnp.where(before, 1.0, 0.0).astype(BF), preferred_element_type=F32)
    chosen = jnp.logical_and(named > 0.0, rank == rank_in)
    one_hot = jnp.where(chosen, 1.0, 0.0)
    pick[0] = one_hot.astype(BF)
    pick[1] = jnp.where(chosen, gates, 0.0).astype(BF)
    for copy in fetch:
        copy.wait()
    ring_first(0, 0)

    def pack(which, rows_ref, out):
        for j in range(4):
            block = jnp.dot(
                pick[which, 192 * j : 192 * (j + 1), :], rows_ref[...], preferred_element_type=F32
            )
            for i in range(8):
                out[8 * j + i] = block[CAP * i : CAP * (i + 1), :].astype(BF)

    def away(n):
        dx, dy, dc = ORDER[n]
        core = c if dc == 0 else 1 - c
        to = (lax.rem(x + dx, NX) * NX + lax.rem(y + dy, NX)) * 2 + core
        source = (lax.rem(x - dx + NX, NX) * NX + lax.rem(y - dy + NX, NX)) * 2 + core
        return to, source

    def dispatch(buf, out, ssem, rsem, lo=0, hi=NE - 1):
        for n in range(lo, hi):
            to = away(n)[0]
            pltpu.make_async_remote_copy(
                src_ref=buf.at[to],
                dst_ref=out.at[e],
                send_sem=ssem.at[n],
                recv_sem=rsem.at[n],
                device_id=(d, to),
                device_id_type=MESH,
            ).start()
        if hi == NE - 1:
            pltpu.make_async_copy(buf.at[e], out.at[e], rsem.at[hi]).start()

    def landed(buf, out, ssem, rsem):
        for n in range(NE - 1):
            to, source = away(n)
            copy = pltpu.make_async_remote_copy(
                src_ref=buf.at[to],
                dst_ref=out.at[source],
                send_sem=ssem.at[n],
                recv_sem=rsem.at[n],
                device_id=(d, to),
                device_id_type=MESH,
            )
            copy.wait_send()
            copy.wait_recv()
        pltpu.make_async_copy(buf.at[e], out.at[e], rsem.at[NE - 1]).wait()

    pack(1, cot_ref, send_cot)
    ring_first(0, 1)
    dispatch(send_cot, cot_out, cot_send_sem, cot_recv_sem, 0, 15)
    acc[...] = jnp.zeros_like(acc)
    w1_out[:, 1408:] = jnp.zeros((1024, 128), BF)
    active[:, 1408:] = jnp.zeros((SLOTS, 128), F32)

    def column(distances):
        for i in distances:
            arrived(col.at[(2 - i) % NZ, e], zp_recv.at[i])

    pos = ((x, y), (y, x))

    def device(h, p, q):
        p, q = lax.rem(p + 2 * NX, NX), lax.rem(q + 2 * NX, NX)
        return (p * NX + q) * 2 + c if h == 0 else (q * NX + p) * 2 + c

    def piece(h, who, sub=None):
        if sub is None:
            return col.at[pl.ds(4 * h, 4), who]
        return col.at[pl.ds(4 * h + 2 * sub, 2), who]

    def share(h, who, n):
        remote(piece(h, who), piece(h, who), mate_send.at[h, n], mate_recv.at[h, n], (d, mate))

    def spread(h, axis, who, n, sub=None, way=None):
        p, q = pos[h]
        for w in (0, 1) if way is None else (way,):
            step = 1 - 2 * w
            to = device(h, p + step, q) if axis == 0 else device(h, p, q + step)
            m = w if sub is None else 2 + w
            remote(
                piece(h, who, sub),
                piece(h, who, sub),
                ax_send.at[h, n, m],
                ax_recv.at[h, n, m],
                (d, to),
            )

    for h in (0, 1):
        column((3, 4, 5, 6) if h else (1, 2, 7))
        p, q = pos[h]
        spread(h, 0, device(h, p, q), 0)
        spread(h, 1, device(h, p, q), 1)
        share(h, device(h, p, q), 0)
    ring_first(1, 0)
    ring_first(1, 1)
    ring_step(0, 0, 0)
    for h in (0, 1):
        p, q = pos[h]
        for w in (0, 1):
            who = device(h, p - 1 + 2 * w, q)
            arrived(piece(h, who), ax_recv.at[h, 0, w])
            spread(h, 0, who, 0, sub=w, way=w)
            spread(h, 1, who, 2 + w)
            share(h, who, 1 + w)
    ring_step(0, 0, 1)
    for h in (0, 1):
        p, q = pos[h]
        who = device(h, p + 2, q)
        for w in (0, 1):
            arrived(piece(h, who, w), ax_recv.at[h, 0, 2 + w])
        spread(h, 1, who, 4)
        share(h, who, 3)
    ring_step(0, 1, 0)

    def second_stage(n):
        for h in (0, 1):
            p, q = pos[h]
            r = p + (0, -1, 1, 2)[n]
            for w in (0, 1):
                who = device(h, r, q - 1 + 2 * w)
                arrived(piece(h, who), ax_recv.at[h, 1 + n, w])
                spread(h, 1, who, 1 + n, sub=w, way=w)
                share(h, who, 4 + 3 * n + w)

    def second_stage_far(h, n):
        p, q = pos[h]
        r = p + (0, -1, 1, 2)[n]
        who = device(h, r, q + 2)
        for w in (0, 1):
            arrived(piece(h, who, w), ax_recv.at[h, 1 + n, 2 + w])
        share(h, who, 6 + 3 * n)

    second_stage(0)
    ring_step(0, 1, 1)
    second_stage(1)
    second_stage(2)
    ring_step(1, 0, 0)
    second_stage(3)
    dispatch(send_cot, cot_out, cot_send_sem, cot_recv_sem, 15)
    ring_step(1, 0, 1)

    def other(h, p, q):
        p, q = lax.rem(p + 2 * NX, NX), lax.rem(q + 2 * NX, NX)
        return ((p * NX + q) if h == 0 else (q * NX + p)) * 2 + (1 - c)

    order = [(0, 0), (-1, 0), (1, 0), (2, 0)]
    for n in range(4):
        r = (0, -1, 1, 2)[n]
        order += [(r, -1), (r, 1), (r, 2)]

    def other_core(h):
        p, q = pos[h]
        for n, (a, b) in enumerate(order):
            arrived(piece(h, other(h, p + a, q + b)), mate_recv.at[h, n])

    def half(n):
        return slice(512 * n, 512 * (n + 1))

    def plane(r):
        return pl.ds(pl.multiple_of(lax.rem(d + r + NZ - 2, NZ) * 512, 512), 512)

    def latent_sum(n, h):
        def step(r, carry):
            block = col[r, :, :, half(n)].reshape(512, 512)
            acc[n] += jnp.dot(tokens_ref[:, plane(r)], block, preferred_element_type=F32)
            return carry

        lax.fori_loop(4 * h, 4 * h + 4, step, 0)

    def latent_half(n):
        latent_sum(n, 1)
        latent = acc[n].astype(BF)
        for j in range(4):
            block = jnp.dot(
                pick[0, 192 * j : 192 * (j + 1), :], latent, preferred_element_type=F32
            )
            for i in range(8):
                send_lat[n, 8 * j + i] = block[CAP * i : CAP * (i + 1), :].astype(BF)
        dispatch(
            send_lat.at[n], lat_out.at[n], lat_send_sem.at[n], lat_recv_sem.at[n]
        )

    for n in range(4):
        second_stage_far(0, n)
    other_core(0)
    for n in (0, 1):
        latent_sum(n, 0)
    for n in range(4):
        second_stage_far(1, n)
    ring_step(1, 1, 0)
    other_core(1)
    latent_half(0)
    ring_step(1, 1, 1)
    latent_half(1)
    ring_step(2, 0, 0)
    ring_step(2, 0, 1)

    def repack(buf, out, columns=slice(None)):
        def go(j, carry):
            pair = jnp.concatenate([buf[2 * j].astype(F32), buf[2 * j + 1].astype(F32)], axis=0)
            out[pl.ds(pl.multiple_of(j * 48, 16), 48), columns] = pair.astype(BF)
            return carry

        lax.fori_loop(0, NE // 2, go, 0)

    ring_step(2, 1, 0)
    ring_step(2, 1, 1)
    ring_step(3, 0, 0)
    ring_step(3, 0, 1)
    own[1].wait()

    def tiles(tile):
        def go(j, carry):
            tile(pl.ds(pl.multiple_of(j * 256, 256), 256))
            return carry

        lax.fori_loop(0, 5, go, 0)
        tile(slice(1280, 1408))

    def latents_in(n):
        landed(send_lat.at[n], lat_out.at[n], lat_send_sem.at[n], lat_recv_sem.at[n])
        repack(lat_out.at[n], rows, half(n))

    def turn(n):
        def go(j, carry):
            part = pl.ds(pl.multiple_of(j * 128, 128), 128)
            rows_t[half(n), part] = rows[part, half(n)].T
            return carry

        lax.fori_loop(0, SLOTS // 128, go, 0)

    def preact_tile(part):
        active[:, part] = jnp.dot(
            rows[:, half(0)], w1_out[half(0), part], preferred_element_type=F32
        )

    def hidden_tile(part):
        preact = active[:, part] + jnp.dot(
            rows[:, half(1)], w1_out[half(1), part], preferred_element_type=F32
        )
        positive = jnp.maximum(preact, 0.0)
        active[:, part] = positive
        hidden_t[part, :] = (positive * positive).astype(BF).T

    def grad_tile(part):
        grad_hidden = contract_last(cots[...], w2_out[part, :])
        grad_pre[:, part] = (grad_hidden * 2.0 * active[:, part]).astype(BF)

    latents_in(0)
    tiles(preact_tile)
    turn(0)
    landed(send_cot, cot_out, cot_send_sem, cot_recv_sem)
    repack(cot_out, cots)
    latents_in(1)
    foremost = (176 * lax.rem(d + 4, NZ)) // 256

    def hidden_turn(j, carry):
        start = lax.rem(foremost + j, 6) * 256
        hidden_tile(pl.ds(pl.multiple_of(start, 256), 256))
        return carry

    lax.fori_loop(0, 2, hidden_turn, 0)

    sums = (
        (sum1_send, sum1_recv, g1_stage, 128),
        (sum2_send, sum2_recv, g2_stage, 176),
    )

    def partial_of(k, owner):
        if k == 0:
            block = rows_t[pl.ds(pl.multiple_of(owner * 128, 128), 128), :]
            return jnp.dot(block, grad_pre[...], preferred_element_type=F32)
        block = hidden_t[pl.ds(pl.multiple_of(owner * 176, 16), 176), :]
        return jnp.dot(block, cots[...], preferred_element_type=F32)

    def sum_copy(s, k, part, way):
        out, inp = sums[k][:2]
        first, count = part_of(k, part)
        span = pl.ds(first, count)
        return pltpu.make_async_remote_copy(
            src_ref=out.at[s, way, span],
            dst_ref=inp.at[s, way, span],
            send_sem=sum_send.at[s, k, part, way],
            recv_sem=sum_recv.at[s, k, part, way],
            device_id=((right if way == 0 else left), e),
            device_id_type=MESH,
        )

    flying = ([], [])

    def sum_send_off(s, k, part, way):
        if len(flying[way]) == DEPTH:
            flying[way].pop(0).wait_send()
        copy = sum_copy(s, k, part, way)
        copy.start()
        flying[way].append(copy)

    def prepare(s, k):
        out, _, stage, _ = sums[k]
        if s == 4:
            stage[...] = partial_of(k, d)
            return
        if s == 0:
            block = partial_of(k, lax.rem(d + 4, NZ)).astype(BF)
            for way in (0, 1):
                first, count = part_of(k, way)
                out[0, way, first : first + count, :] = block[first : first + count, :]
            return
        for way in (0, 1):
            owner = lax.rem(d + 4 - s, NZ) if way == 0 else lax.rem(d + 4 + s, NZ)
            out[s, way] = partial_of(k, owner).astype(BF)

    def push(s, k, late):
        out, inp, stage, _ = sums[k]
        for way in (0, 1):
            part = way if late else 1 - way
            first, count = part_of(k, part)
            span = slice(first, first + count)
            if s > 1 or (s == 1 and late):
                sum_copy(s - 1, k, part, way).wait_recv()
                more = inp[s - 1, way, span, :].astype(F32)
                if s == 4:
                    stage[span, :] += more
                else:
                    out[s, way, span, :] = (out[s, way, span, :].astype(F32) + more).astype(BF)
            if s < 4:
                sum_send_off(s, k, part, way)

    prepare(0, 1)
    push(0, 1, True)
    lax.fori_loop(2, 6, hidden_turn, 0)
    prepare(1, 1)
    push(1, 1, False)
    ring_step(3, 1, 0)
    ring_step(3, 1, 1)
    own[2].wait()
    tiles(grad_tile)
    turn(1)
    prepare(0, 0)
    push(0, 0, True)
    prepare(1, 0)
    push(1, 0, False)
    prepare(2, 1)
    push(1, 1, True)
    push(2, 1, False)

    def route_tile(n, carry):
        part = pl.ds(pl.multiple_of(n * 256, 256), 256)
        block = contract_last(grad_pre[...], w1_out[part, :1408])
        for i in range(NE):
            back_send[i, :, part] = block[CAP * i : CAP * (i + 1), :].astype(BF)
        return carry

    lax.fori_loop(0, 4, route_tile, 0)
    dispatch(back_send, back_recv, back_send_sem, back_recv_sem)
    prepare(2, 0)
    push(1, 0, True)
    push(2, 0, False)
    prepare(3, 1)
    push(2, 1, True)
    push(3, 1, False)
    prepare(3, 0)
    push(2, 0, True)
    push(3, 0, False)
    prepare(4, 1)
    prepare(4, 0)
    push(3, 1, True)
    push(3, 0, True)
    for copy in pending:
        copy.wait_send()
    landed(back_send, back_recv, back_send_sem, back_recv_sem)
    repack(back_recv, rows)
    token_grad = contract_first(pick[0], rows[...]).astype(BF)

    def token_tile(j, carry):
        block = contract_last(token_grad, col[j].reshape(512, 1024))
        tokens_ref[:, plane(j)] = block.astype(BF)
        return carry

    lax.fori_loop(0, NZ, token_tile, 0)
    leave = [pltpu.make_async_copy(tokens_ref, gt_out, local_sem.at[5])]
    leave[0].start()
    push(4, 1, False)
    push(4, 1, True)
    leave.append(pltpu.make_async_copy(g2_stage, g2_out.at[0], local_sem.at[6]))
    leave[1].start()
    push(4, 0, False)
    push(4, 0, True)
    leave.append(pltpu.make_async_copy(g1_stage, g1_out.at[0], local_sem.at[7]))
    leave[2].start()
    for copy in flying[0] + flying[1]:
        copy.wait_send()
    for copy in leave:
        copy.wait()


def layer(tokens, proj, w1, w2, ids, gate, cot):
    anywhere = pl.BlockSpec(memory_space=pl.ANY)
    vmem = pl.BlockSpec(memory_space=pltpu.VMEM)
    dma = pltpu.SemaphoreType.DMA
    slots = (NE, CAP, 1024)
    halves = (2, NE, CAP, 512)
    flat = (SLOTS, 1024)
    results = pl.pallas_call(
        layer_kernel,
        out_shape=(
            jax.ShapeDtypeStruct((128, 4096), BF),
            jax.ShapeDtypeStruct((1, 128, 1408), F32),
            jax.ShapeDtypeStruct((1, 176, 1024), F32),
        ),
        in_specs=[anywhere, anywhere, anywhere, anywhere, vmem, vmem, anywhere],
        out_specs=(anywhere,) * 3,
        scratch_shapes=[
            pltpu.VMEM((NZ, NE, 16, 1024), BF),
            pltpu.VMEM((1024, 1536), BF),
            pltpu.VMEM((1408, 1024), BF),
            pltpu.VMEM(halves, BF),
            pltpu.VMEM(slots, BF),
            pltpu.VMEM((128, 4096), BF),
            pltpu.VMEM((128, 1024), BF),
            pltpu.VMEM((2, SLOTS, 128), BF),
            pltpu.VMEM((2, 128, 512), F32),
            pltpu.VMEM(halves, BF),
            pltpu.VMEM(slots, BF),
            pltpu.VMEM(flat, BF),
            pltpu.VMEM((1024, SLOTS), BF),
            pltpu.VMEM(flat, BF),
            pltpu.VMEM((1536, SLOTS), BF),
            pltpu.VMEM((SLOTS, 1536), F32),
            pltpu.VMEM((SLOTS, 1408), BF),
            pltpu.VMEM(slots, BF),
            pltpu.VMEM(slots, BF),
            pltpu.VMEM((4, 2, 128, 1408), BF),
            pltpu.VMEM((4, 2, 128, 1408), BF),
            pltpu.VMEM((4, 2, 176, 1024), BF),
            pltpu.VMEM((4, 2, 176, 1024), BF),
            pltpu.VMEM((128, 1408), F32),
            pltpu.VMEM((176, 1024), F32),
            dma((NZ,)),
            dma((NZ,)),
            dma((4, 2, 2, 2)),
            dma((4, 2, 2, 2)),
            dma((2, 5, 4)),
            dma((2, 5, 4)),
            dma((2, 16)),
            dma((2, 16)),
            dma((2, NE)),
            dma((2, NE)),
            dma((NE,)),
            dma((NE,)),
            dma((NE,)),
            dma((NE,)),
            dma((4, 2, 2, 2)),
            dma((4, 2, 2, 2)),
            dma((8,)),
        ],
        compiler_params=pltpu.CompilerParams(
            collective_id=0, has_side_effects=True, vmem_limit_bytes=60 * 1024 * 1024
        ),
        name="moe_backward",
    )(tokens, proj, w1, w2, ids.T, gate.T, cot)
    return hand_out(*results)


def hand_kernel(*refs):
    sources, targets, held, sem = refs[:3], refs[3:6], refs[6:9], refs[9]

    def piece(ref, half):
        rows = ref.shape[-2] // 2
        part = pl.ds(half * rows, rows)
        return ref.at[part] if len(ref.shape) == 2 else ref.at[0, part]

    each = [(i, half) for i in range(3) for half in (0, 1)]
    take = [
        pltpu.make_async_copy(piece(sources[i], h), piece(held[i], h), sem.at[0, i, h])
        for i, h in each
    ]
    give = [
        pltpu.make_async_copy(piece(held[i], h), piece(targets[i], h), sem.at[1, i, h])
        for i, h in each
    ]
    for copy in take:
        copy.start()
    for came, goes in zip(take, give):
        came.wait()
        goes.start()
    for copy in give:
        copy.wait()


def hand_out(*results):
    anywhere = pl.BlockSpec(memory_space=pl.ANY)
    return pl.pallas_call(
        hand_kernel,
        out_shape=tuple(jax.ShapeDtypeStruct(a.shape, a.dtype) for a in results),
        in_specs=[anywhere] * 3,
        out_specs=(anywhere,) * 3,
        scratch_shapes=[pltpu.VMEM(a.shape, a.dtype) for a in results]
        + [pltpu.SemaphoreType.DMA((2, 3, 2))],
        compiler_params=pltpu.CompilerParams(vmem_limit_bytes=60 * 1024 * 1024),
        name="hand_out",
    )(*results)


def solution(mesh):
    return jax.shard_map(
        layer,
        mesh=mesh,
        in_specs=(
            P(("dp", "expert"), None),
            P(("dp", "expert"), None),
            P("expert", "dp", None),
            P("expert", "dp", None),
            P(("dp", "expert"), None),
            P(("dp", "expert"), None),
            P(("dp", "expert"), None),
        ),
        out_specs=(P(("dp", "expert"), None), P("expert", "dp", None), P("expert", "dp", None)),
        check_vma=False,
    )
```
